32 devices in a mesh: tc: 16 (over z, y, x), pr: 2 (over core).
Axes of the slice: x: 2, y: 2, z: 4, core: 2. Of those that a mesh axis runs over, the one named last changes fastest.
Arguments:
- pivot_rhs: float32 [16, 1536, 64], P('tc', None, 'pr'), may hold values from -6 to 6
- pivot_inverse: bfloat16 [16, 1536, 1536], P('tc'), as said below
- pivot_owner: int32 [3], replicated, may hold values from 0 to 15, as said below
- coupling_left: bfloat16 [16, 2, 1536, 200], P('tc'), may hold values from -0.15625 to 0.15625
- coupling_right: bfloat16 [16, 2, 1536, 200], P('tc'), may hold values from -0.4375 to 0.4375
- coupling_ranks: int32 [16, 2], P('tc'), may hold values from 100 to 200, as said below
- future_left: bfloat16 [32, 3, 200, 1536], P('tc', None, None, 'pr'), may hold values from -0.15625 to 0.15625
- future_right: bfloat16 [32, 3, 200, 1536], P('tc', None, None, 'pr'), may hold values from -0.4375 to 0.4375
- future_ranks: int32 [32, 3], P('tc'), may hold values from 100 to 200, as said below
- future_rhs: float32 [32, 64, 1536], P('tc', None, 'pr'), may hold values from -6 to 6
Outputs:
- solved: bfloat16 [3, 1536, 64], P(None, None, 'pr')
- future_out: float32 [32, 64, 1536], P('tc', None, 'pr')
The draws below stay inside these ranges and needn't reach their ends.
Inputs may be any that keep to these rules, and one draw needn't show every extreme that they name: `pivot_owner`: the 3 entries are distinct; entry p names the slot, and so the index of tc, that holds pivot p's tiles. `coupling_ranks`: entry [s, j] is the rank of the tile from the pivot in slot s to the pivot j + 1 places later. In every draw a tile that the window uses has rank exactly 200. `future_ranks`: in every draw one of these tiles has rank exactly 200. `pivot_inverse`: each tile is lower triangular.
All inputs are finite; a program needn't handle non-finite values.
Results may differ from the reference program's by a relative error of at most 0.007.
Values may be sent and summed in bfloat16 or wider, within the bound.
No kernel may reach another device: no remote copies, remote signals or barrier semaphores. Data moves between devices by JAX's collectives and lax.ppermute only.
A program may use at most 64 MiB of HBM per device.

```python
import math
import jax
import jax.numpy as jnp
from jax import lax

B = 1536
P_SIZE = 64
R = 200
PIV = 3
FUT = 32
SLOTS = 16


def draw_pivot_inverse(key, part):
    noise_key, diag_key = jax.random.split(jax.random.fold_in(key, 5))
    spread = jax.random.normal(noise_key, (SLOTS, B, B), jnp.float32) * (0.8 / math.sqrt(B))
    diagonal = jax.random.uniform(diag_key, (SLOTS, B), jnp.float32, 0.6, 1.6)
    rows = jnp.arange(B, dtype=jnp.int32)[:, None]
    columns = jnp.arange(B, dtype=jnp.int32)[None, :]
    below = jnp.where(rows > columns, spread, 0.0)
    return jnp.where(rows == columns, diagonal[:, :, None], below).astype(jnp.bfloat16)


def owner_slots(key):
    middle = jax.random.permutation(jax.random.fold_in(key, 21), SLOTS - 2)[:PIV - 2].astype(jnp.int32) + 1
    ends = jnp.array([0, SLOTS - 1], dtype=jnp.int32)
    values = jnp.concatenate([ends, middle])
    order = jax.random.permutation(jax.random.fold_in(key, 22), PIV)
    return values[order].astype(jnp.int32)


def draw_pivot_owner(key, part):
    return owner_slots(key)


def draw_coupling_ranks(key, part):
    owners = owner_slots(key)
    rank_values = jax.random.randint(jax.random.fold_in(key, 11), (SLOTS, PIV - 1), R // 2, R + 1, dtype=jnp.int32)
    return rank_values.at[owners[0], 0].set(R)


def draw_future_ranks(key, part):
    value_key, place_key = jax.random.split(jax.random.fold_in(key, 12))
    rank_values = jax.random.randint(value_key, (FUT * PIV,), R // 2, R + 1, dtype=jnp.int32)
    chosen = jax.random.randint(place_key, (), 0, FUT * PIV, dtype=jnp.int32)
    return rank_values.at[chosen].set(R).reshape(FUT, PIV)


def shard_levels(rng, extent, pieces, least, largest):
    loudness, own = 1.0, jax.random.fold_in(rng, 6)
    for position, blocks in pieces:
        draws = jnp.exp(jax.random.uniform(jax.random.fold_in(own, position), (blocks,), jnp.float32, least / len(pieces), largest / len(pieces)))
        loudness = loudness * jnp.repeat(draws, extent[position] // blocks).reshape([-1 if axis == position else 1 for axis in range(len(extent))])
    return loudness


def noise(key, shape, deviation, reach, cuts=(), kind=jnp.bfloat16):
    values = jax.random.normal(key, shape, jnp.float32) * deviation
    if len(cuts) > 0:
        values = shard_levels(key, shape, cuts, -0.22, 0.18) * values
    return jnp.clip(values, min=-reach, max=reach).astype(kind)


def setup_inputs(seed: int = 0) -> dict:
    keys = jax.random.split(jax.random.key(seed), 11)
    return {
        "pivot_rhs": noise(keys[0], (SLOTS, B, P_SIZE), 1.0, 6.0, ((0, 16), (2, 2)), jnp.float32),
        "pivot_inverse": draw_pivot_inverse(jax.random.fold_in(keys[10], 71), 0),
        "pivot_owner": draw_pivot_owner(jax.random.fold_in(keys[10], 71), 0),
        "coupling_left": noise(keys[3], (SLOTS, PIV - 1, B, R), B ** -0.5, 0.15625, ((0, 16),)),
        "coupling_right": noise(keys[4], (SLOTS, PIV - 1, B, R), R ** -0.5, 0.4375, ((0, 16),)),
        "coupling_ranks": draw_coupling_ranks(jax.random.fold_in(keys[10], 71), 0),
        "future_left": noise(keys[6], (FUT, PIV, R, B), B ** -0.5, 0.15625, ((0, 16), (3, 2))),
        "future_right": noise(keys[7], (FUT, PIV, R, B), R ** -0.5, 0.4375, ((0, 16), (3, 2))),
        "future_ranks": draw_future_ranks(jax.random.fold_in(keys[10], 71), 0),
        "future_rhs": noise(keys[9], (FUT, P_SIZE, B), 1.0, 6.0, ((0, 16), (2, 2)), jnp.float32),
    }


def reference(pivot_rhs, pivot_inverse, pivot_owner, coupling_left, coupling_right, coupling_ranks, future_left, future_right, future_ranks, future_rhs):
    rank_ids = jnp.arange(R, dtype=jnp.int32)
    pending = [pivot_rhs[pivot_owner[tile_id]] for tile_id in range(PIV)]
    solved = [None] * PIV
    for current in reversed(range(PIV)):
        pivot_in = pending[current].astype(jnp.bfloat16)
        solution = jnp.dot(pivot_inverse[pivot_owner[current]].T, pivot_in, preferred_element_type=jnp.float32).astype(jnp.bfloat16)
        solved[current] = solution
        for target in range(current - 1, -1, -1):
            slot_id = pivot_owner[target]
            entry_id = current - target - 1
            factor = jnp.dot(coupling_left[slot_id, entry_id].T, solution, preferred_element_type=jnp.float32)
            factor = jnp.where(rank_ids[:, None] < coupling_ranks[slot_id, entry_id], factor, 0.0).astype(jnp.bfloat16)
            pending[target] = pending[target] - jnp.dot(coupling_right[slot_id, entry_id], factor, preferred_element_type=jnp.float32)
    stacked = jnp.stack(solved)
    solved_wide = stacked.astype(jnp.float32)

    def one_tile(tile_args):
        left_tile, right_tile, tile_ranks, tile_rhs = tile_args
        weights = jnp.einsum("sbq,srb->sqr", solved_wide, left_tile.astype(jnp.float32))
        weights = jnp.where(rank_ids[None, None, :] < tile_ranks[:, None, None], weights, 0.0).astype(jnp.bfloat16)
        return tile_rhs - jnp.einsum("sqr,srb->qb", weights.astype(jnp.float32), right_tile.astype(jnp.float32))

    return stacked, lax.map(one_tile, (future_left, future_right, future_ranks, future_rhs))
```

```python
import functools

import jax
import jax.numpy as jnp
from jax import lax
from jax.sharding import PartitionSpec as P


def doubling_orders(count, cores):
    bits = [1 << place for place in range(count.bit_length() - 1)]
    orders = []
    for core in range(cores):
        order = list(bits)
        if core % 2:
            for place in range(0, len(order) - 1, 2):
                order[place], order[place + 1] = order[place + 1], order[place]
        orders.append(order)
    return orders


def spread(block, slots, cores):
    if slots & (slots - 1):
        return lax.psum(block, "tc")
    orders = doubling_orders(slots, cores)
    for step in range(len(orders[0])):
        pairs = [
            (slot * cores + core, (slot ^ orders[core][step]) * cores + core)
            for slot in range(slots)
            for core in range(cores)
        ]
        block = block + lax.ppermute(block, ("tc", "pr"), pairs)
    return block


def apply_weights(products, right_part, ranks_part):
    rank_ids = lax.broadcasted_iota(jnp.int32, products.shape, 3)
    weights = jnp.where(rank_ids < ranks_part[:, :, None, None], products, 0.0).astype(jnp.bfloat16)
    return jnp.einsum("fsqr,fsrb->fqb", weights, right_part, preferred_element_type=jnp.float32)


def local(
    slots,
    cores,
    pivot_rhs,
    pivot_inverse,
    pivot_owner,
    coupling_left,
    coupling_right,
    coupling_ranks,
    future_left,
    future_right,
    future_ranks,
    future_rhs,
):
    tile_count = pivot_owner.shape[0]
    rank_width = coupling_left.shape[3]
    device_index = lax.axis_index("tc")
    owned_flags = pivot_owner == device_index
    holds_pivot = jnp.any(owned_flags)
    own_pivot = jnp.sum(jnp.where(owned_flags, jnp.arange(tile_count, dtype=jnp.int32), 0))
    pending = pivot_rhs[0]
    inverse_tile = pivot_inverse[0]
    rank_ids = lax.broadcasted_iota(jnp.int32, (rank_width, 1), 0)
    solved = [None] * tile_count
    future_acc = future_rhs
    for current in reversed(range(tile_count)):
        pivot_in = pending.astype(jnp.bfloat16)
        local_solution = lax.dot_general(
            inverse_tile, pivot_in, (((0,), (0,)), ((), ())), preferred_element_type=jnp.float32
        ).astype(jnp.bfloat16)
        is_root = device_index == pivot_owner[current]
        masked_block = jnp.where(is_root, local_solution, jnp.zeros_like(local_solution))
        solved_block = spread(masked_block, slots, cores)
        solved[current] = solved_block
        if current > 0:
            distance = current - own_pivot - 1
            active = jnp.logical_and(holds_pivot, distance >= 0)
            slot_entry = jnp.clip(distance, 0, tile_count - 2)
            left_tile = lax.dynamic_index_in_dim(coupling_left[0], slot_entry, 0, keepdims=False)
            right_tile = lax.dynamic_index_in_dim(coupling_right[0], slot_entry, 0, keepdims=False)
            rank_limit = lax.dynamic_index_in_dim(coupling_ranks[0], slot_entry, 0, keepdims=False)
            factor = lax.dot_general(
                left_tile,
                solved_block,
                (((0,), (0,)), ((), ())),
                preferred_element_type=jnp.float32,
            )
            factor = jnp.where(rank_ids < rank_limit, factor, 0.0).astype(jnp.bfloat16)
            change = jnp.dot(right_tile, factor, preferred_element_type=jnp.float32)
            pending = pending - jnp.where(active, change, 0.0)
    stacked = jnp.stack(solved)
    columns = lax.all_to_all(stacked, "pr", split_axis=1, concat_axis=2, tiled=True)
    products = jnp.einsum(
        "sbq,fsrb->fsqr", columns, future_left, preferred_element_type=jnp.float32
    )
    products = lax.psum(products, "pr")
    future_acc = future_acc - apply_weights(products, future_right, future_ranks)
    return (stacked, future_acc)


def solution(mesh):
    return jax.shard_map(
        functools.partial(local, mesh.shape["tc"], mesh.shape["pr"]),
        mesh=mesh,
        in_specs=(
            P("tc", None, "pr"),
            P("tc", None, None),
            P(),
            P("tc", None, None, None),
            P("tc", None, None, None),
            P("tc", None),
            P("tc", None, None, "pr"),
            P("tc", None, None, "pr"),
            P("tc", None),
            P("tc", None, "pr"),
        ),
        out_specs=(P(None, None, "pr"), P("tc", None, "pr")),
        check_vma=False,
    )
```

```python
import functools

import jax
import jax.numpy as jnp
from jax import lax
from jax.experimental import pallas as pl
from jax.experimental.pallas import tpu as pltpu
from jax.sharding import PartitionSpec as P

SMEM = pl.BlockSpec(memory_space=pltpu.SMEM)
VMEM = pl.BlockSpec(memory_space=pltpu.VMEM)
ANY = pl.BlockSpec(memory_space=pl.ANY)
MIB = 1 << 20


def doubling_orders(count, cores):
    bits = [1 << place for place in range(count.bit_length() - 1)]
    orders = []
    for core in range(cores):
        order = list(bits)
        if core % 2:
            for place in range(0, len(order) - 1, 2):
                order[place], order[place + 1] = order[place + 1], order[place]
        orders.append(order)
    return orders


def spread(block, slots, cores):
    if slots & (slots - 1):
        return lax.psum(block, "tc")
    orders = doubling_orders(slots, cores)
    for step in range(len(orders[0])):
        pairs = [
            (slot * cores + core, (slot ^ orders[core][step]) * cores + core)
            for slot in range(slots)
            for core in range(cores)
        ]
        block = block + lax.ppermute(block, ("tc", "pr"), pairs)
    return block


def swap(block, cores):
    return lax.ppermute(block, "pr", [(core, cores - 1 - core) for core in range(cores)])


def block_width(size):
    return 256 if size % 256 == 0 else size


def start_triangle(inverse_ref, buffer, sems):
    size = inverse_ref.shape[0]
    width = block_width(size)
    copies = []
    for place in range(size // width):
        first = place * width
        part = (pl.ds(first, size - first), pl.ds(first, width))
        copies.append(pltpu.make_async_copy(inverse_ref.at[part], buffer.at[part], sems.at[place]))
    for copy in copies:
        copy.start()
    return copies, width


def first_kernel(owner_ref, rhs_ref, inverse_ref, raw_ref, block_ref, buffer, sems):
    copies, width = start_triangle(inverse_ref, buffer, sems)
    is_root = owner_ref[owner_ref.shape[0] - 1] == lax.axis_index("tc")
    pivot_in = rhs_ref[...].astype(jnp.bfloat16)
    for place, copy in enumerate(copies):
        first = place * width
        copy.wait()
        raw = jnp.dot(
            pivot_in[:, first:], buffer[first:, first : first + width], preferred_element_type=jnp.float32
        )
        raw_ref[:, first : first + width] = raw
        block_ref[:, first : first + width] = jnp.where(is_root, raw, 0.0).astype(jnp.bfloat16)


def ahead_kernel(right_ref, inverse_ref, ahead_ref, buffer, sems):
    copies, width = start_triangle(inverse_ref, buffer, sems)
    for place, copy in enumerate(copies):
        first = place * width
        copy.wait()
        for entry in range(right_ref.shape[0]):
            ahead_ref[entry, :, first : first + width] = jnp.dot(
                right_ref[entry, :, first:],
                buffer[first:, first : first + width],
                preferred_element_type=jnp.float32,
            ).astype(jnp.bfloat16)


def step_kernel(current, owner_ref, ranks_ref, solved_ref, left_ref, ahead_ref, raw_ref, new_raw_ref, block_ref):
    me = lax.axis_index("tc")
    own = jnp.int32(current)
    for place in range(owner_ref.shape[0]):
        own = jnp.where(owner_ref[place] == me, jnp.int32(place), own)
    active = own < current
    entry = jnp.clip(current - own - 1, 0, left_ref.shape[0] - 1)
    limit = jnp.where(active, ranks_ref[0, entry], 0)
    factor = lax.dot_general(
        solved_ref[...], left_ref[entry], (((1,), (1,)), ((), ())), preferred_element_type=jnp.float32
    )
    rank_ids = lax.broadcasted_iota(jnp.int32, factor.shape, 1)
    factor = jnp.where(rank_ids < limit, factor, 0.0).astype(jnp.bfloat16)
    raw = raw_ref[...] - jnp.dot(factor, ahead_ref[entry], preferred_element_type=jnp.float32)
    new_raw_ref[...] = raw
    is_root = owner_ref[current - 1] == me
    block_ref[...] = jnp.where(is_root, raw, 0.0).astype(jnp.bfloat16)


def weights_kernel(pivots, ranks_ref, *refs):
    solved_refs, (own_ref, other_ref, weights_ref) = refs[: len(pivots)], refs[len(pivots) :]
    core = lax.axis_index("pr")
    half = own_ref.shape[3]
    own_rows = pl.ds(pl.multiple_of(core * half, half), half)
    other_rows = pl.ds(pl.multiple_of((1 - core) * half, half), half)
    dims = (((1,), (1,)), ((), ()))
    for place, pivot in enumerate(pivots):
        own_part, other_part = solved_refs[place][:, own_rows], solved_refs[place][:, other_rows]
        for row in range(own_ref.shape[0]):
            products = lax.dot_general(
                own_part, own_ref[row, pivot], dims, preferred_element_type=jnp.float32
            ) + lax.dot_general(other_part, other_ref[row, pivot], dims, preferred_element_type=jnp.float32)
            rank_ids = lax.broadcasted_iota(jnp.int32, products.shape, 1)
            weights_ref[row, place] = jnp.where(rank_ids < ranks_ref[row, pivot], products, 0.0).astype(
                jnp.bfloat16
            )


def update_kernel(pivots, own_ref, other_ref, right_ref, rhs_ref, out_ref):
    core = lax.axis_index("pr")
    probes = own_ref.shape[2]
    for row in range(rhs_ref.shape[0]):
        for ref, slot in ((own_ref, core), (other_ref, 1 - core)):
            rows = pl.ds(pl.multiple_of(slot * probes, probes), probes)
            total = rhs_ref[row, rows, :]
            for place, pivot in enumerate(pivots):
                total = total - jnp.dot(
                    ref[row, place], right_ref[row, pivot], preferred_element_type=jnp.float32
                )
            out_ref[row, rows, :] = total


def call(kernel, shapes, specs, scratch=(), flops=0, read=0, limit=16):
    return pl.pallas_call(
        kernel,
        out_shape=shapes,
        in_specs=specs,
        out_specs=[VMEM] * len(shapes),
        scratch_shapes=list(scratch),
        compiler_params=pltpu.CompilerParams(vmem_limit_bytes=limit * MIB),
        cost_estimate=pl.CostEstimate(flops=flops, bytes_accessed=read, transcendentals=0),
    )


def local(
    slots,
    cores,
    pivot_rhs,
    pivot_inverse,
    pivot_owner,
    coupling_left,
    coupling_right,
    coupling_ranks,
    future_left,
    future_right,
    future_ranks,
    future_rhs,
):
    count = pivot_owner.shape[0]
    size, probes = pivot_rhs.shape[1:]
    rank = coupling_left.shape[3]
    entries = coupling_left.shape[1]
    rows = future_left.shape[0]
    blocks = size // block_width(size)
    inverse = pivot_inverse[0]
    rhs = jnp.swapaxes(pivot_rhs[0], 0, 1)
    left = jnp.swapaxes(coupling_left[0], 1, 2)
    right = jnp.swapaxes(coupling_right[0], 1, 2)
    triangle = [pltpu.VMEM((size, size), jnp.bfloat16), pltpu.SemaphoreType.DMA((blocks,))]
    wide = jax.ShapeDtypeStruct((probes, size), jnp.float32)
    narrow = jax.ShapeDtypeStruct((probes, size), jnp.bfloat16)

    raw, block = call(
        first_kernel, [wide, narrow], [SMEM, VMEM, ANY], triangle, probes * size * size, size * size
    )(pivot_owner, rhs, inverse)
    (ahead,) = call(
        ahead_kernel,
        [jax.ShapeDtypeStruct((entries, rank, size), jnp.bfloat16)],
        [VMEM, ANY],
        triangle,
        entries * rank * size * size,
        size * size + 4 * entries * rank * size,
    )(right, inverse)
    other_left = swap(future_left, cores)

    solved = [None] * count
    for current in reversed(range(count)):
        solved[current] = spread(block, slots, cores)
        if current > 0:
            raw, block = call(
                functools.partial(step_kernel, current),
                [wide, narrow],
                [SMEM, SMEM] + [VMEM] * 4,
                (),
                4 * probes * rank * size,
                4 * rank * size,
            )(pivot_owner, coupling_ranks, solved[current], left, ahead, raw)

    total = future_rhs
    for pivots in (tuple(range(count - 1, 0, -1)), (0,)):
        (weights,) = call(
            functools.partial(weights_kernel, pivots),
            [jax.ShapeDtypeStruct((rows, len(pivots), probes, rank), jnp.bfloat16)],
            [SMEM] + [VMEM] * (len(pivots) + 2),
            (),
            2 * rows * len(pivots) * probes * rank * size,
            2 * rows * len(pivots) * rank * size,
        )(future_ranks, *[solved[pivot] for pivot in pivots], future_left, other_left)
        (total,) = call(
            functools.partial(update_kernel, pivots),
            [jax.ShapeDtypeStruct(total.shape, jnp.float32)],
            [VMEM] * 4,
            (),
            2 * rows * len(pivots) * probes * rank * size,
            rows * len(pivots) * rank * size + 2 * 4 * total.size,
        )(weights, swap(weights, cores), future_right, total)
    return jnp.swapaxes(jnp.stack(solved), 1, 2), total


def solution(mesh):
    return jax.shard_map(
        functools.partial(local, mesh.shape["tc"], mesh.shape["pr"]),
        mesh=mesh,
        in_specs=(
            P("tc", None, "pr"),
            P("tc", None, None),
            P(),
            P("tc", None, None, None),
            P("tc", None, None, None),
            P("tc", None),
            P("tc", None, None, "pr"),
            P("tc", None, None, "pr"),
            P("tc", None),
            P("tc", None, "pr"),
        ),
        out_specs=(P(None, None, "pr"), P("tc", None, "pr")),
        check_vma=False,
    )
```

```python
import functools

import jax
import jax.numpy as jnp
from jax import lax
from jax.experimental import pallas as pl
from jax.experimental.pallas import tpu as pltpu
from jax.sharding import PartitionSpec as P

SMEM = pl.BlockSpec(memory_space=pltpu.SMEM)
VMEM = pl.BlockSpec(memory_space=pltpu.VMEM)
ANY = pl.BlockSpec(memory_space=pl.ANY)
MIB = 1 << 20
FIRST_LIMIT = 56


def exchanges(slots):
    bits = [1 << place for place in range(slots.bit_length() - 1)]
    steps = []
    for place in range(2, len(bits), 2):
        pair = bits[place : place + 2]
        steps.append([(pair[0], pair[-1])])
        if len(pair) == 2:
            steps.append([(pair[1], pair[0])])
    near = bits[:2]
    if len(near) == 2:
        steps.append([(near[0], near[1]), (near[1], near[0]), (near[0] | near[1],) * 2])
    else:
        steps += [[(bit, bit)] for bit in near]
    return steps


def spread(block, slots, cores, beside=()):
    if slots & (slots - 1):
        return lax.psum(block, "tc"), [work() for work in beside]
    done = []
    for step, flips in enumerate(exchanges(slots)):
        received = []
        for flip in flips:
            pairs = [
                (slot * cores + core, (slot ^ flip[core % 2]) * cores + core)
                for slot in range(slots)
                for core in range(cores)
            ]
            received.append(lax.ppermute(block, ("tc", "pr"), pairs))
        if step < len(beside):
            result = beside[step]()
            block, received, result = lax.optimization_barrier((block, received, result))
            done.append(result)
        for part in received:
            block = block + part
    return block, done + [work() for work in beside[len(done) :]]


def swap(block, cores):
    return lax.ppermute(block, "pr", [(core, cores - 1 - core) for core in range(cores)])


def block_width(size):
    return 256 if size % 256 == 0 else size


def start_triangle(inverse_ref, buffer, sems):
    size = inverse_ref.shape[0]
    width = block_width(size)
    copies = []
    for place in range(size // width):
        first = place * width
        part = (pl.ds(first, size - first), pl.ds(first, width))
        copies.append(pltpu.make_async_copy(inverse_ref.at[part], buffer.at[part], sems.at[place]))
    for copy in copies:
        copy.start()
    return copies, width


def first_kernel(owner_ref, rhs_ref, inverse_ref, raw_ref, block_ref, buffer, sems, rhs, owner, more_sems):
    fetch_rhs = pltpu.make_async_copy(rhs_ref, rhs, more_sems.at[0])
    fetch_owner = pltpu.make_async_copy(owner_ref, owner, more_sems.at[1])
    fetch_rhs.start()
    fetch_owner.start()
    copies, width = start_triangle(inverse_ref, buffer, sems)
    fetch_rhs.wait()
    fetch_owner.wait()
    is_root = owner[owner.shape[0] - 1] == lax.axis_index("tc")
    pivot_in = rhs[...].astype(jnp.bfloat16)
    for place, copy in enumerate(copies):
        first = place * width
        copy.wait()
        raw = jnp.dot(
            pivot_in[:, first:], buffer[first:, first : first + width], preferred_element_type=jnp.float32
        )
        raw_ref[:, first : first + width] = raw
        block_ref[:, first : first + width] = jnp.where(is_root, raw, 0.0).astype(jnp.bfloat16)


def ahead_kernel(right_ref, inverse_ref, ahead_ref):
    size = inverse_ref.shape[0]
    width = block_width(size)
    for first in range(0, size, width):
        ahead_ref[:, first : first + width] = jnp.dot(
            right_ref[:, first:], inverse_ref[first:, first : first + width], preferred_element_type=jnp.float32
        ).astype(jnp.bfloat16)


def step_kernel(current, owner_ref, ranks_ref, solved_ref, left_ref, *refs):
    entries = left_ref.shape[0]
    ahead_refs, raw_ref, outs = refs[:entries], refs[entries], refs[entries + 1 :]
    me = lax.axis_index("tc")
    own = jnp.int32(current)
    for place in range(owner_ref.shape[0]):
        own = jnp.where(owner_ref[place] == me, jnp.int32(place), own)
    active = own < current
    is_root = owner_ref[current - 1] == me
    for entry in range(entries):

        @pl.when(jnp.clip(current - own - 1, 0, entries - 1) == entry)
        def _(entry=entry):
            limit = jnp.where(active, ranks_ref[0, entry], 0)
            factor = lax.dot_general(
                solved_ref[...], left_ref[entry], (((1,), (1,)), ((), ())), preferred_element_type=jnp.float32
            )
            rank_ids = lax.broadcasted_iota(jnp.int32, factor.shape, 1)
            factor = jnp.where(rank_ids < limit, factor, 0.0).astype(jnp.bfloat16)
            raw = raw_ref[...] - jnp.dot(factor, ahead_refs[entry][...], preferred_element_type=jnp.float32)
            outs[0][...] = jnp.where(is_root, raw, 0.0).astype(jnp.bfloat16)
            if len(outs) > 1:
                outs[1][...] = raw


def weights_kernel(pivots, ranks_ref, *refs):
    solved_refs, (own_ref, other_ref, weights_ref) = refs[: len(pivots)], refs[len(pivots) :]
    core = lax.axis_index("pr")
    half = own_ref.shape[3]
    own_rows = pl.ds(pl.multiple_of(core * half, half), half)
    other_rows = pl.ds(pl.multiple_of((1 - core) * half, half), half)
    dims = (((1,), (1,)), ((), ()))
    for place, pivot in enumerate(pivots):
        own_part, other_part = solved_refs[place][:, own_rows], solved_refs[place][:, other_rows]
        for row in range(own_ref.shape[0]):
            products = lax.dot_general(
                own_part, own_ref[row, pivot], dims, preferred_element_type=jnp.float32
            ) + lax.dot_general(other_part, other_ref[row, pivot], dims, preferred_element_type=jnp.float32)
            rank_ids = lax.broadcasted_iota(jnp.int32, products.shape, 1)
            weights_ref[row, place] = jnp.where(rank_ids < ranks_ref[row, pivot], products, 0.0).astype(
                jnp.bfloat16
            )


def update_kernel(pivots, own_ref, other_ref, right_ref, rhs_ref, out_ref):
    core = lax.axis_index("pr")
    probes = own_ref.shape[2]
    for row in range(rhs_ref.shape[0]):
        for ref, slot in ((own_ref, core), (other_ref, 1 - core)):
            rows = pl.ds(pl.multiple_of(slot * probes, probes), probes)
            total = rhs_ref[row, rows, :]
            for place, pivot in enumerate(pivots):
                total = total - jnp.dot(
                    ref[row, place], right_ref[row, pivot], preferred_element_type=jnp.float32
                )
            out_ref[row, rows, :] = total


def call(kernel, shapes, specs, scratch=(), flops=0, read=0, limit=16):
    return pl.pallas_call(
        kernel,
        out_shape=shapes,
        in_specs=specs,
        out_specs=[VMEM] * len(shapes),
        scratch_shapes=list(scratch),
        compiler_params=pltpu.CompilerParams(vmem_limit_bytes=limit * MIB),
        cost_estimate=pl.CostEstimate(flops=flops, bytes_accessed=read, transcendentals=0),
    )


def local(
    slots,
    cores,
    pivot_rhs,
    pivot_inverse,
    pivot_owner,
    coupling_left,
    coupling_right,
    coupling_ranks,
    future_left,
    future_right,
    future_ranks,
    future_rhs,
):
    count = pivot_owner.shape[0]
    size, probes = pivot_rhs.shape[1:]
    rank = coupling_left.shape[3]
    entries = coupling_left.shape[1]
    rows = future_left.shape[0]
    blocks = size // block_width(size)
    inverse = pivot_inverse[0]
    rhs = jnp.swapaxes(pivot_rhs[0], 0, 1)
    left = jnp.swapaxes(coupling_left[0], 1, 2)
    right = jnp.swapaxes(coupling_right[0], 1, 2)
    wide = jax.ShapeDtypeStruct((probes, size), jnp.float32)
    narrow = jax.ShapeDtypeStruct((probes, size), jnp.bfloat16)

    raw, block = call(
        first_kernel,
        [wide, narrow],
        [ANY, ANY, ANY],
        [
            pltpu.VMEM((size, size), jnp.bfloat16),
            pltpu.SemaphoreType.DMA((blocks,)),
            pltpu.VMEM((probes, size), jnp.float32),
            pltpu.SMEM((count,), jnp.int32),
            pltpu.SemaphoreType.DMA((2,)),
        ],
        probes * size * size,
        size * size,
        FIRST_LIMIT,
    )(pivot_owner, rhs, inverse)
    block, future_left = lax.optimization_barrier((block, future_left))
    other_left = swap(future_left, cores)

    def ahead(entry):
        return call(
            ahead_kernel,
            [jax.ShapeDtypeStruct((rank, size), jnp.bfloat16)],
            [VMEM, VMEM],
            (),
            rank * size * size,
            size * size + 4 * rank * size,
        )(right[entry], inverse)[0]

    def weigh(*pivots):
        return call(
            functools.partial(weights_kernel, pivots),
            [jax.ShapeDtypeStruct((rows, len(pivots), probes, rank), jnp.bfloat16)],
            [SMEM] + [VMEM] * (len(pivots) + 2),
            (),
            2 * rows * len(pivots) * probes * rank * size,
            2 * rows * len(pivots) * rank * size,
        )(future_ranks, *[solved[pivot] for pivot in pivots], future_left, other_left)[0]

    def update(total, own, other, *pivots):
        return call(
            functools.partial(update_kernel, pivots),
            [jax.ShapeDtypeStruct(total.shape, jnp.float32)],
            [VMEM] * 4,
            (),
            2 * rows * len(pivots) * probes * rank * size,
            rows * len(pivots) * rank * size + 2 * 4 * total.size,
        )(own, other, future_right, total)[0]

    total = future_rhs
    solved = [None] * count
    weights = None
    beside = [functools.partial(ahead, entry) for entry in range(entries)]
    for current in reversed(range(count)):
        solved[current], done = spread(block, slots, cores, beside)
        if current == count - 1:
            factors = done
        else:
            total = done[-1]
        if current > 0:
            last = current == 1
            outs = call(
                functools.partial(step_kernel, current),
                [narrow] if last else [narrow, wide],
                [SMEM, SMEM] + [VMEM] * (entries + 3),
                (),
                4 * probes * rank * size,
                4 * rank * size,
            )(pivot_owner, coupling_ranks, solved[current], left, *factors, raw)
            block = outs[0]
            raw = None if last else outs[1]
            pair = []

            def first_beside(current=current, pair=pair):
                own = weigh(current)
                pair += [own, swap(own, cores)]
                return pair

            def second_beside(current=current, pair=pair, total=total):
                return update(total, pair[0], pair[1], current)

            beside = [first_beside, second_beside]
    own = weigh(0)
    total = update(total, own, swap(own, cores), 0)
    return jnp.swapaxes(jnp.stack(solved), 1, 2), total


def solution(mesh):
    return jax.shard_map(
        functools.partial(local, mesh.shape["tc"], mesh.shape["pr"]),
        mesh=mesh,
        in_specs=(
            P("tc", None, "pr"),
            P("tc", None, None),
            P(),
            P("tc", None, None, None),
            P("tc", None, None, None),
            P("tc", None),
            P("tc", None, None, "pr"),
            P("tc", None, None, "pr"),
            P("tc", None),
            P("tc", None, "pr"),
        ),
        out_specs=(P(None, None, "pr"), P("tc", None, "pr")),
        check_vma=False,
    )
```

```python
import functools

import jax
import jax.numpy as jnp
from jax import lax
from jax.experimental import pallas as pl
from jax.experimental.pallas import tpu as pltpu
from jax.sharding import PartitionSpec as P

SMEM = pl.BlockSpec(memory_space=pltpu.SMEM)
VMEM = pl.BlockSpec(memory_space=pltpu.VMEM)
ANY = pl.BlockSpec(memory_space=pl.ANY)
MIB = 1 << 20
FIRST_LIMIT = 56


def exchanges(slots):
    bits = [1 << place for place in range(slots.bit_length() - 1)]
    groups = [
        [bits[place], bits[place + 1], bits[place] | bits[place + 1]] if place + 1 < len(bits) else [bits[place]]
        for place in range(0, len(bits), 2)
    ]
    others = list(groups)
    for place in range(0, len(groups) - 1, 2):
        if len(groups[place]) == len(groups[place + 1]):
            others[place], others[place + 1] = groups[place + 1], groups[place]
    return [list(zip(group, other)) for group, other in zip(groups, others)]


def spread(block, slots, cores, beside=()):
    if slots & (slots - 1):
        return lax.psum(block, "tc"), [work() for work in beside]
    done = []
    for step, flips in enumerate(exchanges(slots)):
        received = []
        for flip in flips:
            pairs = [
                (slot * cores + core, (slot ^ flip[core % 2]) * cores + core)
                for slot in range(slots)
                for core in range(cores)
            ]
            received.append(lax.ppermute(block, ("tc", "pr"), pairs))
        if step < len(beside):
            result = beside[step]()
            block, received, result = lax.optimization_barrier((block, received, result))
            done.append(result)
        for part in received:
            block = block + part
    return block, done + [work() for work in beside[len(done) :]]


def swap(block, cores):
    return lax.ppermute(block, "pr", [(core, cores - 1 - core) for core in range(cores)])


def block_width(size):
    return 256 if size % 256 == 0 else size


def start_triangle(inverse_ref, buffer, sems):
    size = inverse_ref.shape[0]
    width = block_width(size)
    copies = []
    for place in range(size // width):
        first = place * width
        part = (pl.ds(first, size - first), pl.ds(first, width))
        copies.append(pltpu.make_async_copy(inverse_ref.at[part], buffer.at[part], sems.at[place]))
    for copy in copies:
        copy.start()
    return copies, width


def first_kernel(owner_ref, rhs_ref, inverse_ref, raw_ref, block_ref, buffer, sems, rhs, owner, more_sems):
    fetch_rhs = pltpu.make_async_copy(rhs_ref, rhs, more_sems.at[0])
    fetch_owner = pltpu.make_async_copy(owner_ref, owner, more_sems.at[1])
    fetch_rhs.start()
    fetch_owner.start()
    copies, width = start_triangle(inverse_ref, buffer, sems)
    fetch_rhs.wait()
    fetch_owner.wait()
    is_root = owner[owner.shape[0] - 1] == lax.axis_index("tc")
    pivot_in = rhs[...].astype(jnp.bfloat16)
    for place, copy in enumerate(copies):
        first = place * width
        copy.wait()
        raw = jnp.dot(
            pivot_in[:, first:], buffer[first:, first : first + width], preferred_element_type=jnp.float32
        )
        raw_ref[:, first : first + width] = raw
        block_ref[:, first : first + width] = jnp.where(is_root, raw, 0.0).astype(jnp.bfloat16)


def ahead_kernel(right_ref, inverse_ref, ahead_ref):
    size = inverse_ref.shape[0]
    width = block_width(size)
    for first in range(0, size, width):
        ahead_ref[:, first : first + width] = jnp.dot(
            right_ref[:, first:], inverse_ref[first:, first : first + width], preferred_element_type=jnp.float32
        ).astype(jnp.bfloat16)


def step_kernel(current, owner_ref, ranks_ref, solved_ref, left_ref, *refs):
    entries = left_ref.shape[0]
    ahead_refs, raw_ref, outs = refs[:entries], refs[entries], refs[entries + 1 :]
    me = lax.axis_index("tc")
    own = jnp.int32(current)
    for place in range(owner_ref.shape[0]):
        own = jnp.where(owner_ref[place] == me, jnp.int32(place), own)
    active = own < current
    is_root = owner_ref[current - 1] == me
    for entry in range(entries):

        @pl.when(jnp.clip(current - own - 1, 0, entries - 1) == entry)
        def _(entry=entry):
            limit = jnp.where(active, ranks_ref[0, entry], 0)
            factor = lax.dot_general(
                solved_ref[...], left_ref[entry], (((1,), (1,)), ((), ())), preferred_element_type=jnp.float32
            )
            rank_ids = lax.broadcasted_iota(jnp.int32, factor.shape, 1)
            factor = jnp.where(rank_ids < limit, factor, 0.0).astype(jnp.bfloat16)
            raw = raw_ref[...] - jnp.dot(factor, ahead_refs[entry][...], preferred_element_type=jnp.float32)
            outs[0][...] = jnp.where(is_root, raw, 0.0).astype(jnp.bfloat16)
            if len(outs) > 1:
                outs[1][...] = raw


def weights_kernel(pivots, ranks_ref, *refs):
    solved_refs, (own_ref, other_ref, weights_ref) = refs[: len(pivots)], refs[len(pivots) :]
    core = lax.axis_index("pr")
    half = own_ref.shape[3]
    own_rows = pl.ds(pl.multiple_of(core * half, half), half)
    other_rows = pl.ds(pl.multiple_of((1 - core) * half, half), half)
    dims = (((1,), (1,)), ((), ()))
    for place, pivot in enumerate(pivots):
        own_part, other_part = solved_refs[place][:, own_rows], solved_refs[place][:, other_rows]
        for row in range(own_ref.shape[0]):
            products = lax.dot_general(
                own_part, own_ref[row, pivot], dims, preferred_element_type=jnp.float32
            ) + lax.dot_general(other_part, other_ref[row, pivot], dims, preferred_element_type=jnp.float32)
            rank_ids = lax.broadcasted_iota(jnp.int32, products.shape, 1)
            weights_ref[row, place] = jnp.where(rank_ids < ranks_ref[row, pivot], products, 0.0).astype(
                jnp.bfloat16
            )


def update_kernel(pivots, own_ref, other_ref, right_ref, rhs_ref, out_ref):
    core = lax.axis_index("pr")
    probes = own_ref.shape[2]
    for row in range(rhs_ref.shape[0]):
        for ref, slot in ((own_ref, core), (other_ref, 1 - core)):
            rows = pl.ds(pl.multiple_of(slot * probes, probes), probes)
            total = rhs_ref[row, rows, :]
            for place, pivot in enumerate(pivots):
                total = total - jnp.dot(
                    ref[row, place], right_ref[row, pivot], preferred_element_type=jnp.float32
                )
            out_ref[row, rows, :] = total


def call(kernel, shapes, specs, scratch=(), flops=0, read=0, limit=16):
    return pl.pallas_call(
        kernel,
        out_shape=shapes,
        in_specs=specs,
        out_specs=[VMEM] * len(shapes),
        scratch_shapes=list(scratch),
        compiler_params=pltpu.CompilerParams(vmem_limit_bytes=limit * MIB),
        cost_estimate=pl.CostEstimate(flops=flops, bytes_accessed=read, transcendentals=0),
    )


def local(
    slots,
    cores,
    pivot_rhs,
    pivot_inverse,
    pivot_owner,
    coupling_left,
    coupling_right,
    coupling_ranks,
    future_left,
    future_right,
    future_ranks,
    future_rhs,
):
    count = pivot_owner.shape[0]
    size, probes = pivot_rhs.shape[1:]
    rank = coupling_left.shape[3]
    entries = coupling_left.shape[1]
    rows = future_left.shape[0]
    blocks = size // block_width(size)
    inverse = pivot_inverse[0]
    rhs = jnp.swapaxes(pivot_rhs[0], 0, 1)
    left = jnp.swapaxes(coupling_left[0], 1, 2)
    right = jnp.swapaxes(coupling_right[0], 1, 2)
    wide = jax.ShapeDtypeStruct((probes, size), jnp.float32)
    narrow = jax.ShapeDtypeStruct((probes, size), jnp.bfloat16)

    raw, block = call(
        first_kernel,
        [wide, narrow],
        [ANY, ANY, ANY],
        [
            pltpu.VMEM((size, size), jnp.bfloat16),
            pltpu.SemaphoreType.DMA((blocks,)),
            pltpu.VMEM((probes, size), jnp.float32),
            pltpu.SMEM((count,), jnp.int32),
            pltpu.SemaphoreType.DMA((2,)),
        ],
        probes * size * size,
        size * size,
        FIRST_LIMIT,
    )(pivot_owner, rhs, inverse)
    block, future_left = lax.optimization_barrier((block, future_left))
    other_left = swap(future_left, cores)

    def ahead(entry):
        return call(
            ahead_kernel,
            [jax.ShapeDtypeStruct((rank, size), jnp.bfloat16)],
            [VMEM, VMEM],
            (),
            rank * size * size,
            size * size + 4 * rank * size,
        )(right[entry], inverse)[0]

    def weigh(*pivots):
        return call(
            functools.partial(weights_kernel, pivots),
            [jax.ShapeDtypeStruct((rows, len(pivots), probes, rank), jnp.bfloat16)],
            [SMEM] + [VMEM] * (len(pivots) + 2),
            (),
            2 * rows * len(pivots) * probes * rank * size,
            2 * rows * len(pivots) * rank * size,
        )(future_ranks, *[solved[pivot] for pivot in pivots], future_left, other_left)[0]

    def update(total, own, other, *pivots):
        return call(
            functools.partial(update_kernel, pivots),
            [jax.ShapeDtypeStruct(total.shape, jnp.float32)],
            [VMEM] * 4,
            (),
            2 * rows * len(pivots) * probes * rank * size,
            rows * len(pivots) * rank * size + 2 * 4 * total.size,
        )(own, other, future_right, total)[0]

    total = future_rhs
    solved = [None] * count
    weights = None
    beside = [functools.partial(ahead, entry) for entry in range(entries)]
    for current in reversed(range(count)):
        solved[current], done = spread(block, slots, cores, beside)
        if current == count - 1:
            factors = done
        else:
            total = done[-1]
        if current > 0:
            last = current == 1
            outs = call(
                functools.partial(step_kernel, current),
                [narrow] if last else [narrow, wide],
                [SMEM, SMEM] + [VMEM] * (entries + 3),
                (),
                4 * probes * rank * size,
                4 * rank * size,
            )(pivot_owner, coupling_ranks, solved[current], left, *factors, raw)
            block = outs[0]
            raw = None if last else outs[1]
            pair = []

            def first_beside(current=current, pair=pair):
                own = weigh(current)
                pair += [own, swap(own, cores)]
                return pair

            def second_beside(current=current, pair=pair, total=total):
                return update(total, pair[0], pair[1], current)

            beside = [first_beside, second_beside]
    own = weigh(0)
    total = update(total, own, swap(own, cores), 0)
    return jnp.swapaxes(jnp.stack(solved), 1, 2), total


def solution(mesh):
    return jax.shard_map(
        functools.partial(local, mesh.shape["tc"], mesh.shape["pr"]),
        mesh=mesh,
        in_specs=(
            P("tc", None, "pr"),
            P("tc", None, None),
            P(),
            P("tc", None, None, None),
            P("tc", None, None, None),
            P("tc", None),
            P("tc", None, None, "pr"),
            P("tc", None, None, "pr"),
            P("tc", None),
            P("tc", None, "pr"),
        ),
        out_specs=(P(None, None, "pr"), P("tc", None, "pr")),
        check_vma=False,
    )
```

```python
import functools

import jax
import jax.numpy as jnp
from jax import lax
from jax.experimental import pallas as pl
from jax.experimental.pallas import tpu as pltpu
from jax.sharding import PartitionSpec as P

SMEM = pl.BlockSpec(memory_space=pltpu.SMEM)
VMEM = pl.BlockSpec(memory_space=pltpu.VMEM)
ANY = pl.BlockSpec(memory_space=pl.ANY)
MIB = 1 << 20
FIRST_LIMIT = 56


def exchanges(slots):
    bits = [1 << place for place in range(slots.bit_length() - 1)]
    groups = [
        [bits[place], bits[place + 1], bits[place] | bits[place + 1]] if place + 1 < len(bits) else [bits[place]]
        for place in range(0, len(bits), 2)
    ]
    others = list(groups)
    for place in range(0, len(groups) - 1, 2):
        if len(groups[place]) == len(groups[place + 1]):
            others[place], others[place + 1] = groups[place + 1], groups[place]
    return [list(zip(group, other)) for group, other in zip(groups, others)]


def spread(block, slots, cores, turn, beside=()):
    if slots & (slots - 1):
        for work in beside:
            work()
        return lax.psum(block, "tc")
    beside = list(beside)
    for flips in exchanges(slots):
        received = []
        for flip in flips:
            pairs = [
                (slot * cores + core, (slot ^ flip[(core + turn) % 2]) * cores + core)
                for slot in range(slots)
                for core in range(cores)
            ]
            received.append(lax.ppermute(block, ("tc", "pr"), pairs))
        if beside:
            block, received, _ = lax.optimization_barrier((block, received, beside.pop(0)()))
        for part in received:
            block = block + part
    for work in beside:
        work()
    return block


def swap(block, cores):
    return lax.ppermute(block, "pr", [(core, cores - 1 - core) for core in range(cores)])


def block_width(size):
    return 256 if size % 256 == 0 else size


def start_triangle(inverse_ref, buffer, sems):
    size = inverse_ref.shape[0]
    width = block_width(size)
    copies = []
    for place in range(size // width):
        first = place * width
        part = (pl.ds(first, width), pl.ds(0, first + width))
        copies.append(pltpu.make_async_copy(inverse_ref.at[part], buffer.at[part], sems.at[place]))
    for copy in copies:
        copy.start()
    return copies, width


def first_kernel(owner_ref, rhs_ref, inverse_ref, raw_ref, block_ref, buffer, sems, rhs, owner, more_sems):
    fetch_rhs = pltpu.make_async_copy(rhs_ref, rhs, more_sems.at[0])
    fetch_owner = pltpu.make_async_copy(owner_ref, owner, more_sems.at[1])
    fetch_rhs.start()
    fetch_owner.start()
    copies, width = start_triangle(inverse_ref, buffer, sems)
    fetch_rhs.wait()
    fetch_owner.wait()
    is_root = owner[owner.shape[0] - 1] == lax.axis_index("tc")
    pivot_in = rhs[...].astype(jnp.bfloat16)
    for place, copy in enumerate(copies):
        first = place * width
        copy.wait()
        raw = jnp.dot(
            pivot_in[:, first : first + width], buffer[first : first + width, : first + width], preferred_element_type=jnp.float32
        )
        if place:
            raw_ref[:, :first] += raw[:, :first]
        raw_ref[:, first : first + width] = raw[:, first:]
    block_ref[...] = jnp.where(is_root, raw_ref[...], 0.0).astype(jnp.bfloat16)


def ahead_kernel(
    current, owner_ref, ranks_ref, right_ref, left_ref, inverse_ref, ahead_ref, turned_ref, flag_ref
):
    me = lax.axis_index("tc")
    own = jnp.int32(current)
    for place in range(owner_ref.shape[0]):
        own = jnp.where(owner_ref[place] == me, jnp.int32(place), own)
    entry = jnp.clip(current - own - 1, 0, right_ref.shape[0] - 1)
    limit = jnp.where(own < current, ranks_ref[0, entry], 0)
    size = inverse_ref.shape[0]
    width = block_width(size)
    keep = lax.broadcasted_iota(jnp.int32, (right_ref.shape[1], width), 0) < limit
    for first in range(0, size, width):
        product = jnp.dot(
            right_ref[entry, :, first:], inverse_ref[first:, first : first + width], preferred_element_type=jnp.float32
        )
        ahead_ref[:, first : first + width] = jnp.where(keep, product, 0.0).astype(jnp.bfloat16)
    turned_ref[...] = left_ref[entry].T
    flag_ref[...] = jnp.full(flag_ref.shape, jnp.where(owner_ref[current - 1] == me, 1.0, 0.0), jnp.float32)


def mask_kernel(ranks_ref, right_ref, out_ref):
    rank_ids = lax.broadcasted_iota(jnp.int32, right_ref.shape[2:], 0)
    for row in range(right_ref.shape[0]):
        for pivot in range(right_ref.shape[1]):
            tile = right_ref[row, pivot].astype(jnp.float32)
            out_ref[row, pivot] = jnp.where(rank_ids < ranks_ref[row, pivot], tile, 0.0).astype(jnp.bfloat16)


def step_kernel(solved_ref, ahead_ref, turned_ref, flag_ref, raw_ref, *outs):
    factor = jnp.dot(solved_ref[...], turned_ref[...], preferred_element_type=jnp.float32).astype(jnp.bfloat16)
    raw = raw_ref[...] - jnp.dot(factor, ahead_ref[...], preferred_element_type=jnp.float32)
    outs[0][...] = jnp.where(flag_ref[...] > 0.5, raw, 0.0).astype(jnp.bfloat16)
    if len(outs) > 1:
        outs[1][...] = raw


def weights_kernel(pivot, solved_ref, own_ref, other_ref, weights_ref):
    core = lax.axis_index("pr")
    half = own_ref.shape[3]
    own_part = solved_ref[:, pl.ds(pl.multiple_of(core * half, half), half)]
    other_part = solved_ref[:, pl.ds(pl.multiple_of((1 - core) * half, half), half)]
    dims = (((1,), (1,)), ((), ()))
    for row in range(own_ref.shape[0]):
        weights_ref[row] = (
            lax.dot_general(own_part, own_ref[row, pivot], dims, preferred_element_type=jnp.float32)
            + lax.dot_general(other_part, other_ref[row, pivot], dims, preferred_element_type=jnp.float32)
        ).astype(jnp.bfloat16)


def probe_rows(slot, probes):
    return pl.ds(pl.multiple_of(slot * probes, probes), probes)


def update_kernel(pivot, own_ref, other_ref, right_ref, rhs_ref, out_ref):
    core = lax.axis_index("pr")
    for row in range(rhs_ref.shape[0]):
        for ref, slot in ((own_ref, core), (other_ref, 1 - core)):
            rows = probe_rows(slot, own_ref.shape[1])
            out_ref[row, rows, :] = rhs_ref[row, rows, :] - jnp.dot(
                ref[row], right_ref[row, pivot], preferred_element_type=jnp.float32
            )


def part_update(slot, weights_ref, right_ref, rhs_ref, out_ref, part, sems):
    copies = []
    rows = probe_rows(slot, weights_ref.shape[1])
    for row in range(rhs_ref.shape[0]):
        part[row] = rhs_ref[row, rows, :] - jnp.dot(
            weights_ref[row], right_ref[row, 0], preferred_element_type=jnp.float32
        )
        copies.append(pltpu.make_async_copy(part.at[row], out_ref.at[row, rows, :], sems.at[row]))
        copies[-1].start()
    return copies


def own_kernel(count, weights_ref, right_ref, rhs_ref, *refs):
    solved_refs, (out_ref, stack_ref, part, sems, stack_sems) = refs[:count], refs[count:]
    copies = [
        pltpu.make_async_copy(solved_refs[place], stack_ref.at[place], stack_sems.at[place])
        for place in range(count)
    ]
    for copy in copies:
        copy.start()
    copies += part_update(lax.axis_index("pr"), weights_ref, right_ref, rhs_ref, out_ref, part, sems)
    for copy in copies:
        copy.wait()


def other_kernel(weights_ref, right_ref, rhs_ref, held_ref, out_ref, part, sems):
    del held_ref
    for copy in part_update(1 - lax.axis_index("pr"), weights_ref, right_ref, rhs_ref, out_ref, part, sems):
        copy.wait()


def call(kernel, shapes, specs, scratch=(), flops=0, read=0, limit=16, out=VMEM, aliases=None):
    return pl.pallas_call(
        kernel,
        out_shape=shapes,
        in_specs=specs,
        out_specs=[out] * len(shapes),
        scratch_shapes=list(scratch),
        input_output_aliases=aliases or {},
        compiler_params=pltpu.CompilerParams(vmem_limit_bytes=limit * MIB),
        cost_estimate=pl.CostEstimate(flops=flops, bytes_accessed=read, transcendentals=0),
    )


def local(
    slots,
    cores,
    pivot_rhs,
    pivot_inverse,
    pivot_owner,
    coupling_left,
    coupling_right,
    coupling_ranks,
    future_left,
    future_right,
    future_ranks,
    future_rhs,
):
    count = pivot_owner.shape[0]
    size, probes = pivot_rhs.shape[1:]
    rank = coupling_left.shape[3]
    rows = future_left.shape[0]
    blocks = size // block_width(size)
    inverse = pivot_inverse[0]
    rhs = jnp.swapaxes(pivot_rhs[0], 0, 1)
    left = jnp.swapaxes(coupling_left[0], 1, 2)
    right = jnp.swapaxes(coupling_right[0], 1, 2)
    wide = jax.ShapeDtypeStruct((probes, size), jnp.float32)
    narrow = jax.ShapeDtypeStruct((probes, size), jnp.bfloat16)

    raw, block = call(
        first_kernel,
        [wide, narrow],
        [ANY, ANY, ANY],
        [
            pltpu.VMEM((size, size), jnp.bfloat16),
            pltpu.SemaphoreType.DMA((blocks,)),
            pltpu.VMEM((probes, size), jnp.float32),
            pltpu.SMEM((count,), jnp.int32),
            pltpu.SemaphoreType.DMA((2,)),
        ],
        probes * size * size,
        size * size,
        FIRST_LIMIT,
    )(pivot_owner, rhs, inverse)
    block, future_left = lax.optimization_barrier((block, future_left))
    other_left = swap(future_left, cores)

    def ahead(current):
        return call(
            functools.partial(ahead_kernel, current),
            [
                jax.ShapeDtypeStruct((rank, size), jnp.bfloat16),
                jax.ShapeDtypeStruct((size, rank), jnp.bfloat16),
                jax.ShapeDtypeStruct((1, size), jnp.float32),
            ],
            [SMEM, SMEM, VMEM, VMEM, VMEM],
            (),
            rank * size * size,
            size * size + 4 * rank * size,
        )(pivot_owner, coupling_ranks, right, left, inverse)

    def mask():
        return call(
            mask_kernel,
            [jax.ShapeDtypeStruct(future_right.shape, jnp.bfloat16)],
            [SMEM, VMEM],
            (),
            future_right.size,
            4 * future_right.size,
        )(future_ranks, future_right)[0]

    product_flops = 2 * rows * probes * rank * size

    def weigh(pivot):
        return call(
            functools.partial(weights_kernel, pivot),
            [jax.ShapeDtypeStruct((rows, probes, rank), jnp.bfloat16)],
            [VMEM] * 3,
            (),
            product_flops,
            2 * rows * rank * size,
        )(solved[pivot], future_left, other_left)[0]

    solved = [None] * count
    total = future_rhs
    masked = None
    for current in reversed(range(count)):
        before = current + 1
        held = {}

        def early(current=current, before=before, held=held):
            if before == count:
                held["ready"] = ahead(current) if current > 0 else ()
                return held["ready"]
            held["own"] = weigh(before)
            held["other"] = swap(held["own"], cores)
            if current > 0:
                held["ready"] = ahead(current)
            return held["other"], held.get("ready")

        def late(current=current, before=before, held=held, total=total, masked=masked):
            if before == count:
                return None
            held["masked"] = mask() if masked is None else masked
            held["total"] = call(
                functools.partial(update_kernel, before),
                [jax.ShapeDtypeStruct(total.shape, jnp.float32)],
                [VMEM] * 4,
                (),
                product_flops,
                rows * rank * size + 2 * 4 * total.size,
            )(held["own"], held["other"], held["masked"], total)[0]
            return held["total"]

        solved[current] = spread(block, slots, cores, count - 1 - current, [early, late])
        total, masked = held.get("total", total), held.get("masked", masked)
        if current > 0:
            outs = call(
                step_kernel,
                [narrow, wide] if current > 1 else [narrow],
                [VMEM] * 5,
                (),
                4 * probes * rank * size,
                4 * rank * size,
            )(solved[current], *held["ready"], raw)
            block, raw = outs[0], outs[-1]
    if masked is None:
        masked = mask()
    own = weigh(0)
    other = swap(own, cores)
    half = total.shape[2]
    scratch = [pltpu.VMEM((rows, probes, half), jnp.float32), pltpu.SemaphoreType.DMA((rows,))]
    partial, stacked = call(
        functools.partial(own_kernel, count),
        [
            jax.ShapeDtypeStruct(total.shape, jnp.float32),
            jax.ShapeDtypeStruct((count, probes, size), jnp.bfloat16),
        ],
        [VMEM] * (3 + count),
        scratch + [pltpu.SemaphoreType.DMA((count,))],
        product_flops // 2,
        4 * total.size,
        out=ANY,
    )(own, masked, total, *solved)
    (out,) = call(
        other_kernel,
        [jax.ShapeDtypeStruct(total.shape, jnp.float32)],
        [VMEM] * 3 + [ANY],
        scratch,
        product_flops // 2,
        4 * total.size,
        out=ANY,
        aliases={3: 0},
    )(other, masked, total, partial)
    return jnp.swapaxes(stacked, 1, 2), out


def solution(mesh):
    return jax.shard_map(
        functools.partial(local, mesh.shape["tc"], mesh.shape["pr"]),
        mesh=mesh,
        in_specs=(
            P("tc", None, "pr"),
            P("tc", None, None),
            P(),
            P("tc", None, None, None),
            P("tc", None, None, None),
            P("tc", None),
            P("tc", None, None, "pr"),
            P("tc", None, None, "pr"),
            P("tc", None),
            P("tc", None, "pr"),
        ),
        out_specs=(P(None, None, "pr"), P("tc", None, "pr")),
        check_vma=False,
    )
```

```python
import functools

import jax
import jax.numpy as jnp
from jax import lax
from jax.experimental import pallas as pl
from jax.experimental.pallas import tpu as pltpu
from jax.sharding import PartitionSpec as P

SMEM = pl.BlockSpec(memory_space=pltpu.SMEM)
VMEM = pl.BlockSpec(memory_space=pltpu.VMEM)
ANY = pl.BlockSpec(memory_space=pl.ANY)
MIB = 1 << 20
FIRST_LIMIT = 56


def exchanges(slots):
    bits = [1 << place for place in range(slots.bit_length() - 1)]
    groups = [
        [bits[place], bits[place + 1], bits[place] | bits[place + 1]] if place + 1 < len(bits) else [bits[place]]
        for place in range(0, len(bits), 2)
    ]
    others = list(groups)
    for place in range(0, len(groups) - 1, 2):
        if len(groups[place]) == len(groups[place + 1]):
            others[place], others[place + 1] = groups[place + 1], groups[place]
    return [list(zip(group, other)) for group, other in zip(groups, others)]


def spread(block, slots, cores, turn, beside=()):
    if slots & (slots - 1):
        return lax.psum(block, "tc"), [work() for work in beside]
    beside, done = list(beside), []
    for flips in exchanges(slots):
        received = []
        for flip in flips:
            pairs = [
                (slot * cores + core, (slot ^ flip[(core + turn) % 2]) * cores + core)
                for slot in range(slots)
                for core in range(cores)
            ]
            received.append(lax.ppermute(block, ("tc", "pr"), pairs))
        if beside:
            block, received, result = lax.optimization_barrier((block, received, beside.pop(0)()))
            done.append(result)
        for part in received:
            block = block + part
    return block, done + [work() for work in beside]


def swap(block, cores):
    return lax.ppermute(block, "pr", [(core, cores - 1 - core) for core in range(cores)])


def block_width(size):
    return 256 if size % 256 == 0 else size


def start_triangle(inverse_ref, buffer, sems):
    size = inverse_ref.shape[0]
    width = block_width(size)
    copies = []
    for place in range(size // width):
        first = place * width
        part = (pl.ds(first, width), pl.ds(0, first + width))
        copies.append(pltpu.make_async_copy(inverse_ref.at[part], buffer.at[part], sems.at[place]))
    for copy in copies:
        copy.start()
    return copies, width


def first_kernel(owner_ref, rhs_ref, inverse_ref, raw_ref, block_ref, buffer, sems, rhs, owner, more_sems):
    fetch_rhs = pltpu.make_async_copy(rhs_ref, rhs, more_sems.at[0])
    fetch_owner = pltpu.make_async_copy(owner_ref, owner, more_sems.at[1])
    fetch_rhs.start()
    fetch_owner.start()
    copies, width = start_triangle(inverse_ref, buffer, sems)
    fetch_rhs.wait()
    fetch_owner.wait()
    is_root = owner[owner.shape[0] - 1] == lax.axis_index("tc")
    pivot_in = rhs[...].astype(jnp.bfloat16)
    for place, copy in enumerate(copies):
        first = place * width
        copy.wait()
        raw = jnp.dot(
            pivot_in[:, first : first + width], buffer[first : first + width, : first + width], preferred_element_type=jnp.float32
        )
        if place:
            raw_ref[:, :first] += raw[:, :first]
        raw_ref[:, first : first + width] = raw[:, first:]
    block_ref[...] = jnp.where(is_root, raw_ref[...], 0.0).astype(jnp.bfloat16)


def ahead_kernel(
    current, owner_ref, ranks_ref, right_ref, left_ref, inverse_ref, ahead_ref, turned_ref, flag_ref
):
    me = lax.axis_index("tc")
    own = jnp.int32(current)
    for place in range(owner_ref.shape[0]):
        own = jnp.where(owner_ref[place] == me, jnp.int32(place), own)
    entry = jnp.clip(current - own - 1, 0, right_ref.shape[0] - 1)
    limit = jnp.where(own < current, ranks_ref[0, entry], 0)
    size = inverse_ref.shape[0]
    width = block_width(size)
    keep = lax.broadcasted_iota(jnp.int32, (right_ref.shape[1], width), 0) < limit
    for first in range(0, size, width):
        product = jnp.dot(
            right_ref[entry, :, first:], inverse_ref[first:, first : first + width], preferred_element_type=jnp.float32
        )
        ahead_ref[:, first : first + width] = jnp.where(keep, product, 0.0).astype(jnp.bfloat16)
    turned_ref[...] = left_ref[entry].T
    flag_ref[...] = jnp.full(flag_ref.shape, jnp.where(owner_ref[current - 1] == me, 1.0, 0.0), jnp.float32)


def mask_kernel(ranks_ref, right_ref, out_ref):
    rank_ids = lax.broadcasted_iota(jnp.int32, right_ref.shape[2:], 0)
    for row in range(right_ref.shape[0]):
        for pivot in range(right_ref.shape[1]):
            tile = right_ref[row, pivot].astype(jnp.float32)
            out_ref[row, pivot] = jnp.where(rank_ids < ranks_ref[row, pivot], tile, 0.0).astype(jnp.bfloat16)


def step_kernel(solved_ref, ahead_ref, turned_ref, flag_ref, raw_ref, *outs):
    factor = jnp.dot(solved_ref[...], turned_ref[...], preferred_element_type=jnp.float32).astype(jnp.bfloat16)
    raw = raw_ref[...] - jnp.dot(factor, ahead_ref[...], preferred_element_type=jnp.float32)
    outs[0][...] = jnp.where(flag_ref[...] > 0.5, raw, 0.0).astype(jnp.bfloat16)
    if len(outs) > 1:
        outs[1][...] = raw


def weights_kernel(pivot, solved_ref, own_ref, other_ref, weights_ref):
    core = lax.axis_index("pr")
    half = own_ref.shape[3]
    own_part = solved_ref[:, pl.ds(pl.multiple_of(core * half, half), half)]
    other_part = solved_ref[:, pl.ds(pl.multiple_of((1 - core) * half, half), half)]
    dims = (((1,), (1,)), ((), ()))
    for row in range(own_ref.shape[0]):
        weights_ref[row] = (
            lax.dot_general(own_part, own_ref[row, pivot], dims, preferred_element_type=jnp.float32)
            + lax.dot_general(other_part, other_ref[row, pivot], dims, preferred_element_type=jnp.float32)
        ).astype(jnp.bfloat16)


def probe_rows(slot, probes):
    return pl.ds(pl.multiple_of(slot * probes, probes), probes)


def update_kernel(pivot, own_ref, other_ref, right_ref, rhs_ref, out_ref):
    core = lax.axis_index("pr")
    for row in range(rhs_ref.shape[0]):
        for ref, slot in ((own_ref, core), (other_ref, 1 - core)):
            rows = probe_rows(slot, own_ref.shape[1])
            out_ref[row, rows, :] = rhs_ref[row, rows, :] - jnp.dot(
                ref[row], right_ref[row, pivot], preferred_element_type=jnp.float32
            )


def part_update(slot, weights_ref, right_ref, rhs_ref, out_ref, part, sems):
    copies = []
    rows = probe_rows(slot, weights_ref.shape[1])
    for row in range(rhs_ref.shape[0]):
        part[row] = rhs_ref[row, rows, :] - jnp.dot(
            weights_ref[row], right_ref[row, 0], preferred_element_type=jnp.float32
        )
        copies.append(pltpu.make_async_copy(part.at[row], out_ref.at[row, rows, :], sems.at[row]))
        copies[-1].start()
    return copies


def own_kernel(count, weights_ref, right_ref, rhs_ref, *refs):
    solved_refs, (out_ref, stack_ref, part, sems, stack_sems) = refs[:count], refs[count:]
    copies = [
        pltpu.make_async_copy(solved_refs[place], stack_ref.at[place], stack_sems.at[place])
        for place in range(count)
    ]
    for copy in copies:
        copy.start()
    copies += part_update(lax.axis_index("pr"), weights_ref, right_ref, rhs_ref, out_ref, part, sems)
    for copy in copies:
        copy.wait()


def other_kernel(weights_ref, right_ref, rhs_ref, held_ref, out_ref, part, sems):
    del held_ref
    for copy in part_update(1 - lax.axis_index("pr"), weights_ref, right_ref, rhs_ref, out_ref, part, sems):
        copy.wait()


def call(kernel, shapes, specs, scratch=(), flops=0, read=0, limit=16, out=VMEM, aliases=None):
    return pl.pallas_call(
        kernel,
        out_shape=shapes,
        in_specs=specs,
        out_specs=[out] * len(shapes),
        scratch_shapes=list(scratch),
        input_output_aliases=aliases or {},
        compiler_params=pltpu.CompilerParams(vmem_limit_bytes=limit * MIB),
        cost_estimate=pl.CostEstimate(flops=flops, bytes_accessed=read, transcendentals=0),
    )


def local(
    slots,
    cores,
    pivot_rhs,
    pivot_inverse,
    pivot_owner,
    coupling_left,
    coupling_right,
    coupling_ranks,
    future_left,
    future_right,
    future_ranks,
    future_rhs,
):
    count = pivot_owner.shape[0]
    size, probes = pivot_rhs.shape[1:]
    rank = coupling_left.shape[3]
    rows = future_left.shape[0]
    blocks = size // block_width(size)
    inverse = pivot_inverse[0]
    rhs = jnp.swapaxes(pivot_rhs[0], 0, 1)
    left = jnp.swapaxes(coupling_left[0], 1, 2)
    right = jnp.swapaxes(coupling_right[0], 1, 2)
    wide = jax.ShapeDtypeStruct((probes, size), jnp.float32)
    narrow = jax.ShapeDtypeStruct((probes, size), jnp.bfloat16)

    raw, block = call(
        first_kernel,
        [wide, narrow],
        [ANY, ANY, ANY],
        [
            pltpu.VMEM((size, size), jnp.bfloat16),
            pltpu.SemaphoreType.DMA((blocks,)),
            pltpu.VMEM((probes, size), jnp.float32),
            pltpu.SMEM((count,), jnp.int32),
            pltpu.SemaphoreType.DMA((2,)),
        ],
        probes * size * size,
        size * size,
        FIRST_LIMIT,
    )(pivot_owner, rhs, inverse)

    def ahead(current):
        return call(
            functools.partial(ahead_kernel, current),
            [
                jax.ShapeDtypeStruct((rank, size), jnp.bfloat16),
                jax.ShapeDtypeStruct((size, rank), jnp.bfloat16),
                jax.ShapeDtypeStruct((1, size), jnp.float32),
            ],
            [SMEM, SMEM, VMEM, VMEM, VMEM],
            (),
            rank * size * size,
            size * size + 4 * rank * size,
        )(pivot_owner, coupling_ranks, right, left, inverse)

    def mask():
        return call(
            mask_kernel,
            [jax.ShapeDtypeStruct(future_right.shape, jnp.bfloat16)],
            [SMEM, VMEM],
            (),
            future_right.size,
            4 * future_right.size,
        )(future_ranks, future_right)[0]

    product_flops = 2 * rows * probes * rank * size

    def weigh(pivot):
        return call(
            functools.partial(weights_kernel, pivot),
            [jax.ShapeDtypeStruct((rows, probes, rank), jnp.bfloat16)],
            [VMEM] * 3,
            (),
            product_flops,
            2 * rows * rank * size,
        )(solved[pivot], future_left, halves["other"])[0]

    solved = [None] * count
    total = future_rhs
    masked = None
    halves = {}
    for current in reversed(range(count)):
        before = current + 1
        held = {}

        def early(current=current, before=before, held=held):
            if before == count:
                held["ready"] = ahead(current) if current > 0 else ()
                return held["ready"], future_left
            held["own"] = weigh(before)
            held["other"] = swap(held["own"], cores)
            if current > 0:
                held["ready"] = ahead(current)
            return held["other"], held.get("ready")

        def late(current=current, before=before, held=held, total=total, masked=masked):
            if before == count:
                return None
            held["masked"] = mask() if masked is None else masked
            held["total"] = call(
                functools.partial(update_kernel, before),
                [jax.ShapeDtypeStruct(total.shape, jnp.float32)],
                [VMEM] * 4,
                (),
                product_flops,
                rows * rank * size + 2 * 4 * total.size,
            )(held["own"], held["other"], held["masked"], total)[0]
            return held["total"]

        solved[current], done = spread(block, slots, cores, count - 1 - current, [early, late])
        if before == count:
            halves["other"] = swap(done[0][1], cores)
        total, masked = held.get("total", total), held.get("masked", masked)
        if current > 0:
            outs = call(
                step_kernel,
                [narrow, wide] if current > 1 else [narrow],
                [VMEM] * 5,
                (),
                4 * probes * rank * size,
                4 * rank * size,
            )(solved[current], *held["ready"], raw)
            block, raw = outs[0], outs[-1]
    if masked is None:
        masked = mask()
    own = weigh(0)
    other = swap(own, cores)
    half = total.shape[2]
    scratch = [pltpu.VMEM((rows, probes, half), jnp.float32), pltpu.SemaphoreType.DMA((rows,))]
    partial, stacked = call(
        functools.partial(own_kernel, count),
        [
            jax.ShapeDtypeStruct(total.shape, jnp.float32),
            jax.ShapeDtypeStruct((count, probes, size), jnp.bfloat16),
        ],
        [VMEM] * (3 + count),
        scratch + [pltpu.SemaphoreType.DMA((count,))],
        product_flops // 2,
        4 * total.size,
        out=ANY,
    )(own, masked, total, *solved)
    (out,) = call(
        other_kernel,
        [jax.ShapeDtypeStruct(total.shape, jnp.float32)],
        [VMEM] * 3 + [ANY],
        scratch,
        product_flops // 2,
        4 * total.size,
        out=ANY,
        aliases={3: 0},
    )(other, masked, total, partial)
    return jnp.swapaxes(stacked, 1, 2), out


def solution(mesh):
    return jax.shard_map(
        functools.partial(local, mesh.shape["tc"], mesh.shape["pr"]),
        mesh=mesh,
        in_specs=(
            P("tc", None, "pr"),
            P("tc", None, None),
            P(),
            P("tc", None, None, None),
            P("tc", None, None, None),
            P("tc", None),
            P("tc", None, None, "pr"),
            P("tc", None, None, "pr"),
            P("tc", None),
            P("tc", None, "pr"),
        ),
        out_specs=(P(None, None, "pr"), P("tc", None, "pr")),
        check_vma=False,
    )
```

```python
import functools

import jax
import jax.numpy as jnp
from jax import lax
from jax.experimental import pallas as pl
from jax.experimental.pallas import tpu as pltpu
from jax.sharding import PartitionSpec as P

SMEM = pl.BlockSpec(memory_space=pltpu.SMEM)
VMEM = pl.BlockSpec(memory_space=pltpu.VMEM)
ANY = pl.BlockSpec(memory_space=pl.ANY)
MIB = 1 << 20
FIRST_LIMIT = 56


def exchanges(slots):
    bits = [1 << place for place in range(slots.bit_length() - 1)]
    groups = [
        [bits[place], bits[place + 1], bits[place] | bits[place + 1]] if place + 1 < len(bits) else [bits[place]]
        for place in range(0, len(bits), 2)
    ]
    others = list(groups)
    for place in range(0, len(groups) - 1, 2):
        if len(groups[place]) == len(groups[place + 1]):
            others[place], others[place + 1] = groups[place + 1], groups[place]
    return [list(zip(group, other)) for group, other in zip(groups, others)]


def spread(block, slots, cores, turn, beside=()):
    if slots & (slots - 1):
        for work in beside:
            work()
        return [lax.psum(block, "tc")]
    parts = [block]
    beside = list(beside)
    for flips in exchanges(slots):
        block = functools.reduce(jnp.add, parts)
        received = []
        for flip in flips:
            pairs = [
                (slot * cores + core, (slot ^ flip[(core + turn) % 2]) * cores + core)
                for slot in range(slots)
                for core in range(cores)
            ]
            received.append(lax.ppermute(block, ("tc", "pr"), pairs))
        if beside:
            block, received, _ = lax.optimization_barrier((block, received, beside.pop(0)()))
        parts = [block, *received]
    for work in beside:
        work()
    return parts


def swap(block, cores):
    return lax.ppermute(block, "pr", [(core, cores - 1 - core) for core in range(cores)])


def block_width(size):
    return 256 if size % 256 == 0 else size


def start_triangle(inverse_ref, buffer, sems):
    size = inverse_ref.shape[0]
    width = block_width(size)
    copies = []
    for place in range(size // width):
        first = place * width
        part = (pl.ds(first, width), pl.ds(0, first + width))
        copies.append(pltpu.make_async_copy(inverse_ref.at[part], buffer.at[part], sems.at[place]))
    for copy in copies:
        copy.start()
    return copies, width


def first_kernel(owner_ref, rhs_ref, inverse_ref, raw_ref, block_ref, buffer, sems, rhs, owner, more_sems):
    fetch_rhs = pltpu.make_async_copy(rhs_ref, rhs, more_sems.at[0])
    fetch_owner = pltpu.make_async_copy(owner_ref, owner, more_sems.at[1])
    fetch_rhs.start()
    fetch_owner.start()
    copies, width = start_triangle(inverse_ref, buffer, sems)
    fetch_rhs.wait()
    fetch_owner.wait()
    is_root = owner[owner.shape[0] - 1] == lax.axis_index("tc")
    pivot_in = rhs[...].astype(jnp.bfloat16)
    for place, copy in enumerate(copies):
        first = place * width
        copy.wait()
        raw = jnp.dot(
            pivot_in[:, first : first + width], buffer[first : first + width, : first + width], preferred_element_type=jnp.float32
        )
        if place:
            raw_ref[:, :first] += raw[:, :first]
        raw_ref[:, first : first + width] = raw[:, first:]
    block_ref[...] = jnp.where(is_root, raw_ref[...], 0.0).astype(jnp.bfloat16)


def ahead_kernel(
    current, owner_ref, ranks_ref, right_ref, left_ref, inverse_ref, ahead_ref, turned_ref, flag_ref
):
    me = lax.axis_index("tc")
    own = jnp.int32(current)
    for place in range(owner_ref.shape[0]):
        own = jnp.where(owner_ref[place] == me, jnp.int32(place), own)
    entry = jnp.clip(current - own - 1, 0, right_ref.shape[0] - 1)
    limit = jnp.where(own < current, ranks_ref[0, entry], 0)
    size = inverse_ref.shape[0]
    width = block_width(size)
    keep = lax.broadcasted_iota(jnp.int32, (right_ref.shape[1], width), 0) < limit
    for first in range(0, size, width):
        product = jnp.dot(
            right_ref[entry, :, first:], inverse_ref[first:, first : first + width], preferred_element_type=jnp.float32
        )
        ahead_ref[:, first : first + width] = jnp.where(keep, product, 0.0).astype(jnp.bfloat16)
    turned_ref[...] = left_ref[entry].T
    flag_ref[...] = jnp.full(flag_ref.shape, jnp.where(owner_ref[current - 1] == me, 1.0, 0.0), jnp.float32)


def mask_kernel(ranks_ref, right_ref, out_ref):
    rank_ids = lax.broadcasted_iota(jnp.int32, right_ref.shape[2:], 0)
    for row in range(right_ref.shape[0]):
        for pivot in range(right_ref.shape[1]):
            tile = right_ref[row, pivot].astype(jnp.float32)
            out_ref[row, pivot] = jnp.where(rank_ids < ranks_ref[row, pivot], tile, 0.0).astype(jnp.bfloat16)


def sum_of(part_refs):
    return functools.reduce(jnp.add, [ref[...] for ref in part_refs])


def step_kernel(count, *refs):
    ahead_ref, turned_ref, flag_ref, raw_ref, solved_ref, *outs = refs[count:]
    solved = sum_of(refs[:count])
    solved_ref[...] = solved
    factor = jnp.dot(solved, turned_ref[...], preferred_element_type=jnp.float32).astype(jnp.bfloat16)
    raw = raw_ref[...] - jnp.dot(factor, ahead_ref[...], preferred_element_type=jnp.float32)
    outs[0][...] = jnp.where(flag_ref[...] > 0.5, raw, 0.0).astype(jnp.bfloat16)
    if len(outs) > 1:
        outs[1][...] = raw


def weights_kernel(pivot, solved_ref, own_ref, other_ref, weights_ref):
    core = lax.axis_index("pr")
    half = own_ref.shape[3]
    own_part = solved_ref[:, pl.ds(pl.multiple_of(core * half, half), half)]
    other_part = solved_ref[:, pl.ds(pl.multiple_of((1 - core) * half, half), half)]
    dims = (((1,), (1,)), ((), ()))
    for row in range(own_ref.shape[0]):
        weights_ref[row] = (
            lax.dot_general(own_part, own_ref[row, pivot], dims, preferred_element_type=jnp.float32)
            + lax.dot_general(other_part, other_ref[row, pivot], dims, preferred_element_type=jnp.float32)
        ).astype(jnp.bfloat16)


def turn_kernel(own_ref, other_ref, own_out_ref, other_out_ref):
    for row in range(own_ref.shape[0]):
        own_out_ref[row] = own_ref[row, 0].T
        other_out_ref[row] = other_ref[row, 0].T


def last_weights_kernel(count, *refs):
    own_ref, other_ref, weights_ref, solved_ref = refs[count:]
    solved_ref[...] = sum_of(refs[:count])
    core = lax.axis_index("pr")
    half = own_ref.shape[1]
    own_part = solved_ref[:, pl.ds(pl.multiple_of(core * half, half), half)]
    other_part = solved_ref[:, pl.ds(pl.multiple_of((1 - core) * half, half), half)]
    for row in range(own_ref.shape[0]):
        weights_ref[row] = (
            jnp.dot(own_part, own_ref[row], preferred_element_type=jnp.float32)
            + jnp.dot(other_part, other_ref[row], preferred_element_type=jnp.float32)
        ).astype(jnp.bfloat16)


def probe_rows(slot, probes):
    return pl.ds(pl.multiple_of(slot * probes, probes), probes)


def update_kernel(pivot, own_ref, other_ref, right_ref, rhs_ref, out_ref):
    core = lax.axis_index("pr")
    for row in range(rhs_ref.shape[0]):
        for ref, slot in ((own_ref, core), (other_ref, 1 - core)):
            rows = probe_rows(slot, own_ref.shape[1])
            out_ref[row, rows, :] = rhs_ref[row, rows, :] - jnp.dot(
                ref[row], right_ref[row, pivot], preferred_element_type=jnp.float32
            )


def part_update(slot, weights_ref, right_ref, rhs_ref, out_ref, part, sems):
    copies = []
    rows = probe_rows(slot, weights_ref.shape[1])
    for row in range(rhs_ref.shape[0]):
        part[row] = rhs_ref[row, rows, :] - jnp.dot(
            weights_ref[row], right_ref[row, 0], preferred_element_type=jnp.float32
        )
        copies.append(pltpu.make_async_copy(part.at[row], out_ref.at[row, rows, :], sems.at[row]))
        copies[-1].start()
    return copies


def own_kernel(count, weights_ref, right_ref, rhs_ref, *refs):
    solved_refs, (out_ref, stack_ref, part, sems, stack_sems) = refs[:count], refs[count:]
    copies = [
        pltpu.make_async_copy(solved_refs[place], stack_ref.at[place], stack_sems.at[place])
        for place in range(count)
    ]
    for copy in copies:
        copy.start()
    copies += part_update(lax.axis_index("pr"), weights_ref, right_ref, rhs_ref, out_ref, part, sems)
    for copy in copies:
        copy.wait()


def other_kernel(weights_ref, right_ref, rhs_ref, held_ref, out_ref, part, sems):
    del held_ref
    for copy in part_update(1 - lax.axis_index("pr"), weights_ref, right_ref, rhs_ref, out_ref, part, sems):
        copy.wait()


def call(kernel, shapes, specs, scratch=(), flops=0, read=0, limit=16, out=VMEM, aliases=None):
    return pl.pallas_call(
        kernel,
        out_shape=shapes,
        in_specs=specs,
        out_specs=[out] * len(shapes),
        scratch_shapes=list(scratch),
        input_output_aliases=aliases or {},
        compiler_params=pltpu.CompilerParams(vmem_limit_bytes=limit * MIB),
        cost_estimate=pl.CostEstimate(flops=flops, bytes_accessed=read, transcendentals=0),
    )


def local(
    slots,
    cores,
    pivot_rhs,
    pivot_inverse,
    pivot_owner,
    coupling_left,
    coupling_right,
    coupling_ranks,
    future_left,
    future_right,
    future_ranks,
    future_rhs,
):
    count = pivot_owner.shape[0]
    size, probes = pivot_rhs.shape[1:]
    rank = coupling_left.shape[3]
    rows = future_left.shape[0]
    blocks = size // block_width(size)
    inverse = pivot_inverse[0]
    rhs = jnp.swapaxes(pivot_rhs[0], 0, 1)
    left = jnp.swapaxes(coupling_left[0], 1, 2)
    right = jnp.swapaxes(coupling_right[0], 1, 2)
    wide = jax.ShapeDtypeStruct((probes, size), jnp.float32)
    narrow = jax.ShapeDtypeStruct((probes, size), jnp.bfloat16)

    raw, block = call(
        first_kernel,
        [wide, narrow],
        [ANY, ANY, ANY],
        [
            pltpu.VMEM((size, size), jnp.bfloat16),
            pltpu.SemaphoreType.DMA((blocks,)),
            pltpu.VMEM((probes, size), jnp.float32),
            pltpu.SMEM((count,), jnp.int32),
            pltpu.SemaphoreType.DMA((2,)),
        ],
        probes * size * size,
        size * size,
        FIRST_LIMIT,
    )(pivot_owner, rhs, inverse)
    block, future_left = lax.optimization_barrier((block, future_left))
    other_left = swap(future_left, cores)

    def ahead(current):
        return call(
            functools.partial(ahead_kernel, current),
            [
                jax.ShapeDtypeStruct((rank, size), jnp.bfloat16),
                jax.ShapeDtypeStruct((size, rank), jnp.bfloat16),
                jax.ShapeDtypeStruct((1, size), jnp.float32),
            ],
            [SMEM, SMEM, VMEM, VMEM, VMEM],
            (),
            rank * size * size,
            size * size + 4 * rank * size,
        )(pivot_owner, coupling_ranks, right, left, inverse)

    def mask():
        return call(
            mask_kernel,
            [jax.ShapeDtypeStruct(future_right.shape, jnp.bfloat16)],
            [SMEM, VMEM],
            (),
            future_right.size,
            4 * future_right.size,
        )(future_ranks, future_right)[0]

    product_flops = 2 * rows * probes * rank * size

    def weigh(pivot):
        return call(
            functools.partial(weights_kernel, pivot),
            [jax.ShapeDtypeStruct((rows, probes, rank), jnp.bfloat16)],
            [VMEM] * 3,
            (),
            product_flops,
            2 * rows * rank * size,
        )(solved[pivot], future_left, other_left)[0]

    def turn():
        half = future_left.shape[3]
        return call(
            turn_kernel,
            [jax.ShapeDtypeStruct((rows, half, rank), jnp.bfloat16)] * 2,
            [VMEM] * 2,
            (),
            rows * rank * size,
            4 * rows * rank * size,
        )(future_left, other_left)

    turned = []
    solved = [None] * count
    total = future_rhs
    masked = None
    for current in reversed(range(count)):
        before = current + 1
        held = {}

        def early(current=current, before=before, held=held):
            if before == count:
                held["ready"] = ahead(current) if current > 0 else ()
                return held["ready"]
            held["own"] = weigh(before)
            held["other"] = swap(held["own"], cores)
            if current > 0:
                held["ready"] = ahead(current)
            return held["other"], held.get("ready")

        def late(current=current, before=before, held=held, total=total, masked=masked):
            if before == count:
                return None
            held["masked"] = mask() if masked is None else masked
            if not turned:
                turned.extend(turn())
            held["total"] = call(
                functools.partial(update_kernel, before),
                [jax.ShapeDtypeStruct(total.shape, jnp.float32)],
                [VMEM] * 4,
                (),
                product_flops,
                rows * rank * size + 2 * 4 * total.size,
            )(held["own"], held["other"], held["masked"], total)[0]
            return held["total"], list(turned)

        parts = spread(block, slots, cores, count - 1 - current, [early, late])
        total, masked = held.get("total", total), held.get("masked", masked)
        if current > 0:
            outs = call(
                functools.partial(step_kernel, len(parts)),
                [narrow, narrow, wide] if current > 1 else [narrow, narrow],
                [VMEM] * (len(parts) + 4),
                (),
                4 * probes * rank * size,
                4 * rank * size,
            )(*parts, *held["ready"], raw)
            solved[current], block, raw = outs[0], outs[1], outs[-1]
    if masked is None:
        masked = mask()
    if not turned:
        turned.extend(turn())
    own, solved[0] = call(
        functools.partial(last_weights_kernel, len(parts)),
        [jax.ShapeDtypeStruct((rows, probes, rank), jnp.bfloat16), narrow],
        [VMEM] * (len(parts) + 2),
        (),
        product_flops,
        2 * rows * rank * size,
    )(*parts, *turned)
    other = swap(own, cores)
    half = total.shape[2]
    scratch = [pltpu.VMEM((rows, probes, half), jnp.float32), pltpu.SemaphoreType.DMA((rows,))]
    partial, stacked = call(
        functools.partial(own_kernel, count),
        [
            jax.ShapeDtypeStruct(total.shape, jnp.float32),
            jax.ShapeDtypeStruct((count, probes, size), jnp.bfloat16),
        ],
        [VMEM] * (3 + count),
        scratch + [pltpu.SemaphoreType.DMA((count,))],
        product_flops // 2,
        4 * total.size,
        out=ANY,
    )(own, masked, total, *solved)
    (out,) = call(
        other_kernel,
        [jax.ShapeDtypeStruct(total.shape, jnp.float32)],
        [VMEM] * 3 + [ANY],
        scratch,
        product_flops // 2,
        4 * total.size,
        out=ANY,
        aliases={3: 0},
    )(other, masked, total, partial)
    return jnp.swapaxes(stacked, 1, 2), out


def solution(mesh):
    return jax.shard_map(
        functools.partial(local, mesh.shape["tc"], mesh.shape["pr"]),
        mesh=mesh,
        in_specs=(
            P("tc", None, "pr"),
            P("tc", None, None),
            P(),
            P("tc", None, None, None),
            P("tc", None, None, None),
            P("tc", None),
            P("tc", None, None, "pr"),
            P("tc", None, None, "pr"),
            P("tc", None),
            P("tc", None, "pr"),
        ),
        out_specs=(P(None, None, "pr"), P("tc", None, "pr")),
        check_vma=False,
    )
```

```python
import functools

import jax
import jax.numpy as jnp
from jax import lax
from jax.experimental import pallas as pl
from jax.experimental.pallas import tpu as pltpu
from jax.sharding import PartitionSpec as P

SMEM = pl.BlockSpec(memory_space=pltpu.SMEM)
VMEM = pl.BlockSpec(memory_space=pltpu.VMEM)
ANY = pl.BlockSpec(memory_space=pl.ANY)
MIB = 1 << 20
FIRST_LIMIT = 56


def exchanges(slots):
    bits = [1 << place for place in range(slots.bit_length() - 1)]
    groups = [
        [bits[place], bits[place + 1], bits[place] | bits[place + 1]] if place + 1 < len(bits) else [bits[place]]
        for place in range(0, len(bits), 2)
    ]
    others = list(groups)
    for place in range(0, len(groups) - 1, 2):
        if len(groups[place]) == len(groups[place + 1]):
            others[place], others[place + 1] = groups[place + 1], groups[place]
    return [list(zip(group, other)) for group, other in zip(groups, others)]


def spread(block, slots, cores, turn, beside=()):
    if slots & (slots - 1):
        for work in beside:
            work()
        return [lax.psum(block, "tc")]
    parts = [block]
    beside = list(beside)
    for flips in exchanges(slots):
        block = functools.reduce(jnp.add, parts)
        received = []
        for flip in flips:
            pairs = [
                (slot * cores + core, (slot ^ flip[(core + turn) % 2]) * cores + core)
                for slot in range(slots)
                for core in range(cores)
            ]
            received.append(lax.ppermute(block, ("tc", "pr"), pairs))
        if beside:
            block, received, _ = lax.optimization_barrier((block, received, beside.pop(0)()))
        parts = [block, *received]
    for work in beside:
        work()
    return parts


def swap(block, cores):
    return lax.ppermute(block, "pr", [(core, cores - 1 - core) for core in range(cores)])


def block_width(size):
    return 256 if size % 256 == 0 else size


def start_triangle(inverse_ref, buffer, sems):
    size = inverse_ref.shape[0]
    width = block_width(size)
    copies = []
    for place in range(size // width):
        first = place * width
        part = (pl.ds(first, width), pl.ds(0, first + width))
        copies.append(pltpu.make_async_copy(inverse_ref.at[part], buffer.at[part], sems.at[place]))
    for copy in copies:
        copy.start()
    return copies, width


def first_kernel(owner_ref, rhs_ref, inverse_ref, raw_ref, block_ref, buffer, sems, rhs, owner, more_sems):
    fetch_rhs = pltpu.make_async_copy(rhs_ref, rhs, more_sems.at[0])
    fetch_owner = pltpu.make_async_copy(owner_ref, owner, more_sems.at[1])
    fetch_rhs.start()
    fetch_owner.start()
    copies, width = start_triangle(inverse_ref, buffer, sems)
    fetch_rhs.wait()
    fetch_owner.wait()
    is_root = owner[owner.shape[0] - 1] == lax.axis_index("tc")
    pivot_in = rhs[...].astype(jnp.bfloat16)
    for place, copy in enumerate(copies):
        first = place * width
        copy.wait()
        raw = jnp.dot(
            pivot_in[:, first : first + width], buffer[first : first + width, : first + width], preferred_element_type=jnp.float32
        )
        if place:
            raw_ref[:, :first] += raw[:, :first]
        raw_ref[:, first : first + width] = raw[:, first:]
    block_ref[...] = jnp.where(is_root, raw_ref[...], 0.0).astype(jnp.bfloat16)


def ahead_kernel(
    current, owner_ref, ranks_ref, right_ref, left_ref, inverse_ref, ahead_ref, turned_ref, flag_ref
):
    me = lax.axis_index("tc")
    own = jnp.int32(current)
    for place in range(owner_ref.shape[0]):
        own = jnp.where(owner_ref[place] == me, jnp.int32(place), own)
    entry = jnp.clip(current - own - 1, 0, right_ref.shape[0] - 1)
    limit = jnp.where(own < current, ranks_ref[0, entry], 0)
    size = inverse_ref.shape[0]
    width = block_width(size)
    keep = lax.broadcasted_iota(jnp.int32, (right_ref.shape[1], width), 0) < limit
    for first in range(0, size, width):
        product = jnp.dot(
            right_ref[entry, :, first:], inverse_ref[first:, first : first + width], preferred_element_type=jnp.float32
        )
        ahead_ref[:, first : first + width] = jnp.where(keep, product, 0.0).astype(jnp.bfloat16)
    turned_ref[...] = left_ref[entry].T
    flag_ref[...] = jnp.full(flag_ref.shape, jnp.where(owner_ref[current - 1] == me, 1.0, 0.0), jnp.float32)


def mask_kernel(ranks_ref, right_ref, out_ref):
    rank_ids = lax.broadcasted_iota(jnp.int32, right_ref.shape[2:], 0)
    for row in range(right_ref.shape[0]):
        for pivot in range(right_ref.shape[1]):
            tile = right_ref[row, pivot].astype(jnp.float32)
            out_ref[row, pivot] = jnp.where(rank_ids < ranks_ref[row, pivot], tile, 0.0).astype(jnp.bfloat16)


def sum_of(part_refs):
    return functools.reduce(jnp.add, [ref[...] for ref in part_refs])


def step_kernel(count, *refs):
    ahead_ref, turned_ref, flag_ref, raw_ref, solved_ref, *outs = refs[count:]
    solved = sum_of(refs[:count])
    solved_ref[...] = solved
    factor = jnp.dot(solved, turned_ref[...], preferred_element_type=jnp.float32).astype(jnp.bfloat16)
    raw = raw_ref[...] - jnp.dot(factor, ahead_ref[...], preferred_element_type=jnp.float32)
    outs[0][...] = jnp.where(flag_ref[...] > 0.5, raw, 0.0).astype(jnp.bfloat16)
    if len(outs) > 1:
        outs[1][...] = raw


def weights_kernel(pivot, solved_ref, own_ref, other_ref, weights_ref):
    core = lax.axis_index("pr")
    half = own_ref.shape[3]
    own_part = solved_ref[:, pl.ds(pl.multiple_of(core * half, half), half)]
    other_part = solved_ref[:, pl.ds(pl.multiple_of((1 - core) * half, half), half)]
    dims = (((1,), (1,)), ((), ()))
    for row in range(own_ref.shape[0]):
        weights_ref[row] = (
            lax.dot_general(own_part, own_ref[row, pivot], dims, preferred_element_type=jnp.float32)
            + lax.dot_general(other_part, other_ref[row, pivot], dims, preferred_element_type=jnp.float32)
        ).astype(jnp.bfloat16)


def turn_kernel(own_ref, other_ref, own_out_ref, other_out_ref):
    for row in range(own_ref.shape[0]):
        own_out_ref[row] = own_ref[row, 0].T
        other_out_ref[row] = other_ref[row, 0].T


def last_weights_kernel(count, *refs):
    own_ref, other_ref, weights_ref, solved_ref = refs[count:]
    solved_ref[...] = sum_of(refs[:count])
    core = lax.axis_index("pr")
    half = own_ref.shape[1]
    own_part = solved_ref[:, pl.ds(pl.multiple_of(core * half, half), half)]
    other_part = solved_ref[:, pl.ds(pl.multiple_of((1 - core) * half, half), half)]
    for row in range(own_ref.shape[0]):
        weights_ref[row] = (
            jnp.dot(own_part, own_ref[row], preferred_element_type=jnp.float32)
            + jnp.dot(other_part, other_ref[row], preferred_element_type=jnp.float32)
        ).astype(jnp.bfloat16)


def probe_rows(slot, probes):
    return pl.ds(pl.multiple_of(slot * probes, probes), probes)


def update_kernel(pivot, own_ref, other_ref, right_ref, rhs_ref, out_ref):
    core = lax.axis_index("pr")
    for row in range(rhs_ref.shape[0]):
        for ref, slot in ((own_ref, core), (other_ref, 1 - core)):
            rows = probe_rows(slot, own_ref.shape[1])
            out_ref[row, rows, :] = rhs_ref[row, rows, :] - jnp.dot(
                ref[row], right_ref[row, pivot], preferred_element_type=jnp.float32
            )


def part_update(slot, weights_ref, right_ref, rhs_ref, out_ref, part, sems):
    copies = []
    probes = weights_ref.shape[1]
    rows = probe_rows(slot, probes)
    width = rhs_ref.shape[2] // 2
    for row in range(rhs_ref.shape[0]):
        for half in range(2):
            cols = pl.ds(half * width, width)
            part[row, :, cols] = rhs_ref[row, rows, cols] - jnp.dot(
                weights_ref[row], right_ref[row, 0, :, cols], preferred_element_type=jnp.float32
            )
            copies.append(pltpu.make_async_copy(part.at[row, :, cols], out_ref.at[row, rows, cols], sems.at[2 * row + half]))
            copies[-1].start()
    return copies


def own_kernel(count, weights_ref, right_ref, rhs_ref, *refs):
    solved_refs, (out_ref, stack_ref, part, sems, stack_sems) = refs[:count], refs[count:]
    copies = [
        pltpu.make_async_copy(solved_refs[place], stack_ref.at[place], stack_sems.at[place])
        for place in range(count)
    ]
    for copy in copies:
        copy.start()
    copies += part_update(lax.axis_index("pr"), weights_ref, right_ref, rhs_ref, out_ref, part, sems)
    for copy in copies:
        copy.wait()


def other_kernel(weights_ref, right_ref, rhs_ref, held_ref, out_ref, part, sems):
    del held_ref
    for copy in part_update(1 - lax.axis_index("pr"), weights_ref, right_ref, rhs_ref, out_ref, part, sems):
        copy.wait()


def call(kernel, shapes, specs, scratch=(), flops=0, read=0, limit=16, out=VMEM, aliases=None):
    return pl.pallas_call(
        kernel,
        out_shape=shapes,
        in_specs=specs,
        out_specs=[out] * len(shapes),
        scratch_shapes=list(scratch),
        input_output_aliases=aliases or {},
        compiler_params=pltpu.CompilerParams(vmem_limit_bytes=limit * MIB),
        cost_estimate=pl.CostEstimate(flops=flops, bytes_accessed=read, transcendentals=0),
    )


def local(
    slots,
    cores,
    pivot_rhs,
    pivot_inverse,
    pivot_owner,
    coupling_left,
    coupling_right,
    coupling_ranks,
    future_left,
    future_right,
    future_ranks,
    future_rhs,
):
    count = pivot_owner.shape[0]
    size, probes = pivot_rhs.shape[1:]
    rank = coupling_left.shape[3]
    rows = future_left.shape[0]
    blocks = size // block_width(size)
    inverse = pivot_inverse[0]
    rhs = jnp.swapaxes(pivot_rhs[0], 0, 1)
    left = jnp.swapaxes(coupling_left[0], 1, 2)
    right = jnp.swapaxes(coupling_right[0], 1, 2)
    wide = jax.ShapeDtypeStruct((probes, size), jnp.float32)
    narrow = jax.ShapeDtypeStruct((probes, size), jnp.bfloat16)

    raw, block = call(
        first_kernel,
        [wide, narrow],
        [ANY, ANY, ANY],
        [
            pltpu.VMEM((size, size), jnp.bfloat16),
            pltpu.SemaphoreType.DMA((blocks,)),
            pltpu.VMEM((probes, size), jnp.float32),
            pltpu.SMEM((count,), jnp.int32),
            pltpu.SemaphoreType.DMA((2,)),
        ],
        probes * size * size,
        size * size,
        FIRST_LIMIT,
    )(pivot_owner, rhs, inverse)
    block, future_left = lax.optimization_barrier((block, future_left))
    other_left = swap(future_left, cores)

    def ahead(current):
        return call(
            functools.partial(ahead_kernel, current),
            [
                jax.ShapeDtypeStruct((rank, size), jnp.bfloat16),
                jax.ShapeDtypeStruct((size, rank), jnp.bfloat16),
                jax.ShapeDtypeStruct((1, size), jnp.float32),
            ],
            [SMEM, SMEM, VMEM, VMEM, VMEM],
            (),
            rank * size * size,
            size * size + 4 * rank * size,
        )(pivot_owner, coupling_ranks, right, left, inverse)

    def mask():
        return call(
            mask_kernel,
            [jax.ShapeDtypeStruct(future_right.shape, jnp.bfloat16)],
            [SMEM, VMEM],
            (),
            future_right.size,
            4 * future_right.size,
        )(future_ranks, future_right)[0]

    product_flops = 2 * rows * probes * rank * size

    def weigh(pivot):
        return call(
            functools.partial(weights_kernel, pivot),
            [jax.ShapeDtypeStruct((rows, probes, rank), jnp.bfloat16)],
            [VMEM] * 3,
            (),
            product_flops,
            2 * rows * rank * size,
        )(solved[pivot], future_left, other_left)[0]

    def turn():
        half = future_left.shape[3]
        return call(
            turn_kernel,
            [jax.ShapeDtypeStruct((rows, half, rank), jnp.bfloat16)] * 2,
            [VMEM] * 2,
            (),
            rows * rank * size,
            4 * rows * rank * size,
        )(future_left, other_left)

    turned = []
    solved = [None] * count
    total = future_rhs
    masked = None
    for current in reversed(range(count)):
        before = current + 1
        held = {}

        def early(current=current, before=before, held=held):
            if before == count:
                held["ready"] = ahead(current) if current > 0 else ()
                return held["ready"]
            held["own"] = weigh(before)
            held["other"] = swap(held["own"], cores)
            if current > 0:
                held["ready"] = ahead(current)
            return held["other"], held.get("ready")

        def late(current=current, before=before, held=held, total=total, masked=masked):
            if before == count:
                return None
            held["masked"] = mask() if masked is None else masked
            if not turned:
                turned.extend(turn())
            held["total"] = call(
                functools.partial(update_kernel, before),
                [jax.ShapeDtypeStruct(total.shape, jnp.float32)],
                [VMEM] * 4,
                (),
                product_flops,
                rows * rank * size + 2 * 4 * total.size,
            )(held["own"], held["other"], held["masked"], total)[0]
            return held["total"], list(turned)

        parts = spread(block, slots, cores, count - 1 - current, [early, late])
        total, masked = held.get("total", total), held.get("masked", masked)
        if current > 0:
            outs = call(
                functools.partial(step_kernel, len(parts)),
                [narrow, narrow, wide] if current > 1 else [narrow, narrow],
                [VMEM] * (len(parts) + 4),
                (),
                4 * probes * rank * size,
                4 * rank * size,
            )(*parts, *held["ready"], raw)
            solved[current], block, raw = outs[0], outs[1], outs[-1]
    if masked is None:
        masked = mask()
    if not turned:
        turned.extend(turn())
    own, solved[0] = call(
        functools.partial(last_weights_kernel, len(parts)),
        [jax.ShapeDtypeStruct((rows, probes, rank), jnp.bfloat16), narrow],
        [VMEM] * (len(parts) + 2),
        (),
        product_flops,
        2 * rows * rank * size,
    )(*parts, *turned)
    other = swap(own, cores)
    half = total.shape[2]
    scratch = [pltpu.VMEM((rows, probes, half), jnp.float32), pltpu.SemaphoreType.DMA((2 * rows,))]
    partial, stacked = call(
        functools.partial(own_kernel, count),
        [
            jax.ShapeDtypeStruct(total.shape, jnp.float32),
            jax.ShapeDtypeStruct((count, probes, size), jnp.bfloat16),
        ],
        [VMEM] * (3 + count),
        scratch + [pltpu.SemaphoreType.DMA((count,))],
        product_flops // 2,
        4 * total.size,
        out=ANY,
    )(own, masked, total, *solved)
    (out,) = call(
        other_kernel,
        [jax.ShapeDtypeStruct(total.shape, jnp.float32)],
        [VMEM] * 3 + [ANY],
        scratch,
        product_flops // 2,
        4 * total.size,
        out=ANY,
        aliases={3: 0},
    )(other, masked, total, partial)
    return jnp.swapaxes(stacked, 1, 2), out


def solution(mesh):
    return jax.shard_map(
        functools.partial(local, mesh.shape["tc"], mesh.shape["pr"]),
        mesh=mesh,
        in_specs=(
            P("tc", None, "pr"),
            P("tc", None, None),
            P(),
            P("tc", None, None, None),
            P("tc", None, None, None),
            P("tc", None),
            P("tc", None, None, "pr"),
            P("tc", None, None, "pr"),
            P("tc", None),
            P("tc", None, "pr"),
        ),
        out_specs=(P(None, None, "pr"), P("tc", None, "pr")),
        check_vma=False,
    )
```
